256 devices in a mesh: tile: 32 (over z_lo, y, core), sample: 8 (over x, z_hi).
Axes of the slice: x: 4, y: 4, z: 8 (z_hi: 2, z_lo: 4; z = z_hi * 4 + z_lo), core: 2. Of those that a mesh axis runs over, the one named last changes fastest.
Arguments:
- inputs: bfloat16 [8, 16, 32, 1024], P('sample', None, 'tile'), may hold values from -6 to 6
- first_weight: bfloat16 [9, 1024, 1024], P(None, 'tile'), may hold values from -0.0625 to 0.0625
- second_weight: bfloat16 [9, 1024, 1024], P(None, 'tile'), may hold values from -0.0625 to 0.0625
- norm_gain_vector: float32 [1024], P('tile'), may hold values from 0.5 to 1.5
- norm_bias: float32 [1024], P('tile'), may hold values from -3 to 3
- cotangent: bfloat16 [8, 16, 32, 1024], P('sample', None, 'tile'), may hold values from -6 to 6
Outputs:
- input_grad: bfloat16 [8, 16, 32, 1024], P('sample', None, 'tile')
- first_grad: float32 [9, 1024, 1024], P(None, 'tile')
- second_grad: float32 [9, 1024, 1024], P(None, None, 'tile')
- gain_gradient: float32 [1024], P('tile')
- shift_grad: float32 [1024], P('tile')
The draws below stay inside these ranges and needn't reach their ends.
All inputs are finite; a program needn't handle non-finite values.
Results may differ from the reference program's by a relative error of at most 0.0044.
Values may be sent and summed in bfloat16 or wider, within the bound.
No kernel may reach another device: no remote copies, remote signals or barrier semaphores. Data moves between devices by JAX's collectives and lax.ppermute only.
A program may use at most 64 MiB of HBM per device.

```python
import jax
import jax.numpy as jnp
from jax import lax

CHANNEL_COUNT = 1024
NORM_GROUPS = 32
BAND_ROWS = 16
BAND_COLUMNS = 32
IMAGE_COUNT = 8
GROUP_CHANNELS = 32


def block_scale(key, shape, shards, low, largest):
    def one(axis_at, parts):
        steps = jax.random.uniform(jax.random.fold_in(jax.random.fold_in(key, 6), axis_at), (parts,), jnp.float32, low / len(shards), largest / len(shards))
        return jnp.repeat(jnp.exp(steps), shape[axis_at] // parts).reshape((-1,) + (1,) * (len(shape) - axis_at - 1))

    gain = one(*shards[0])
    for cut in shards[1:]:
        gain = gain * one(*cut)
    return gain


def centred(rng, shape, deviation, bound, split=(), held_as=jnp.bfloat16):
    array = jax.random.normal(rng, shape, jnp.float32) * deviation
    if len(split) > 0:
        array = block_scale(rng, shape, split, -0.22, 0.18) * array
    return jnp.clip(array, min=-bound, max=bound).astype(held_as)


def setup_inputs(seed: int = 0) -> dict:
    arg_keys = jax.random.split(jax.random.key(seed), 7)
    return {
        "inputs": centred(arg_keys[0], (IMAGE_COUNT, BAND_ROWS, BAND_COLUMNS, CHANNEL_COUNT), 1.0, 6.0, ((0, 8), (2, 32))),
        "first_weight": centred(arg_keys[1], (9, CHANNEL_COUNT, CHANNEL_COUNT), (9 * CHANNEL_COUNT) ** -0.5, 0.0625, ((1, 32),)),
        "second_weight": centred(arg_keys[2], (9, CHANNEL_COUNT, CHANNEL_COUNT), (9 * CHANNEL_COUNT) ** -0.5, 0.0625, ((1, 32),)),
        "norm_gain_vector": jnp.clip(1.0 + 0.1 * jax.random.normal(arg_keys[3], (CHANNEL_COUNT,), jnp.float32), 0.5, 1.5),
        "norm_bias": centred(arg_keys[4], (CHANNEL_COUNT,), 0.5, 3.0, ((0, 32),), jnp.float32),
        "cotangent": centred(arg_keys[5], (IMAGE_COUNT, BAND_ROWS, BAND_COLUMNS, CHANNEL_COUNT), 1.0, 6.0, ((0, 8), (2, 32))),
    }


OFFSETS = [(row_step, col_step) for row_step in (-1, 0, 1) for col_step in (-1, 0, 1)]

def shift_grid(block, row_step, col_step):
    padded = jnp.pad(block, ((0, 0), (1, 1), (1, 1), (0, 0)))
    return padded[:, 1 + row_step:1 + row_step + block.shape[1], 1 + col_step:1 + col_step + block.shape[2], :]

def reference(inputs, first_weight, second_weight, norm_gain_vector, norm_bias, cotangent):
    element_count = IMAGE_COUNT * BAND_ROWS * BAND_COLUMNS
    grid = (IMAGE_COUNT, BAND_ROWS, BAND_COLUMNS, CHANNEL_COUNT)
    pre = jnp.zeros((element_count, CHANNEL_COUNT), jnp.float32)
    for tap, (row_step, col_step) in enumerate(OFFSETS):
        moved = shift_grid(inputs, row_step, col_step).reshape(element_count, CHANNEL_COUNT)
        pre = pre + jnp.dot(moved, first_weight[tap].T, preferred_element_type=jnp.float32)
    group_view = pre.reshape(IMAGE_COUNT, BAND_ROWS * BAND_COLUMNS, NORM_GROUPS, GROUP_CHANNELS)
    group_mean = lax.optimization_barrier(jnp.mean(group_view, axis=(1, 3), keepdims=True))
    variance = lax.optimization_barrier(jnp.mean((group_view - group_mean) ** 2, axis=(1, 3), keepdims=True))
    inverse_deviation = lax.rsqrt(variance + 1e-05)
    standardized_input = ((group_view - group_mean) * inverse_deviation).reshape(element_count, CHANNEL_COUNT)
    normalized_output = standardized_input * norm_gain_vector + norm_bias
    sig = jax.nn.sigmoid(normalized_output)
    act = (normalized_output * sig).astype(jnp.bfloat16).reshape(grid)
    dy_rows = cotangent.reshape(element_count, CHANNEL_COUNT)
    second_grad = jnp.stack([jnp.dot(dy_rows.T, shift_grid(act, rs, cs).reshape(element_count, CHANNEL_COUNT), preferred_element_type=jnp.float32) for rs, cs in OFFSETS])
    act_grad = jnp.zeros(grid, jnp.float32)
    for tap, (row_step, col_step) in enumerate(OFFSETS):
        term = jnp.dot(dy_rows, second_weight[tap], preferred_element_type=jnp.float32).reshape(grid)
        act_grad = act_grad + shift_grid(term, -row_step, -col_step)
    normed_gradient = act_grad.reshape(element_count, CHANNEL_COUNT) * sig * (1.0 + normalized_output * (1.0 - sig))
    gain_gradient = lax.optimization_barrier(jnp.sum(normed_gradient * standardized_input, axis=0))
    shift_grad = lax.optimization_barrier(jnp.sum(normed_gradient, axis=0))
    scaled = (normed_gradient * norm_gain_vector).reshape(IMAGE_COUNT, BAND_ROWS * BAND_COLUMNS, NORM_GROUPS, GROUP_CHANNELS)
    input_groups = standardized_input.reshape(IMAGE_COUNT, BAND_ROWS * BAND_COLUMNS, NORM_GROUPS, GROUP_CHANNELS)
    first_mean = lax.optimization_barrier(jnp.mean(scaled, axis=(1, 3), keepdims=True))
    second_mean = lax.optimization_barrier(jnp.mean(scaled * input_groups, axis=(1, 3), keepdims=True))
    pre_grad = (inverse_deviation * (scaled - first_mean - input_groups * second_mean)).astype(jnp.bfloat16).reshape(element_count, CHANNEL_COUNT)
    first_grad = jnp.stack([jnp.dot(pre_grad.T, shift_grid(inputs, rs, cs).reshape(element_count, CHANNEL_COUNT), preferred_element_type=jnp.float32) for rs, cs in OFFSETS])
    conv_back = jnp.zeros(grid, jnp.float32)
    for tap, (row_step, col_step) in enumerate(OFFSETS):
        term = jnp.dot(pre_grad, first_weight[tap], preferred_element_type=jnp.float32).reshape(grid)
        conv_back = conv_back + shift_grid(term, -row_step, -col_step)
    conv_back = conv_back.astype(jnp.bfloat16)
    input_grad = (cotangent.astype(jnp.float32) + conv_back.astype(jnp.float32)).astype(jnp.bfloat16)
    return (input_grad, first_grad, second_grad, gain_gradient, shift_grad)
```

```python
import functools

import jax
import jax.numpy as jnp
from jax import lax
from jax.experimental import pallas as pl
from jax.experimental.pallas import tpu as pltpu
from jax.sharding import PartitionSpec as P

BF = jnp.bfloat16
F32 = jnp.float32
TAPS = [(dr, dc) for dr in (-1, 0, 1) for dc in (-1, 0, 1)]
ROWS, COLS, CH = 16, 32, 1024
POS = ROWS * COLS
OWN = 32
MB = 1 << 20

Z_MASKS, Y_MASKS, CORE = (8, 16, 24), (2, 4, 6), 1
ORDER = [c ^ y ^ z for c in (0, 1) for y in (0, 2, 4, 6) for z in (0, 8, 16, 24)]
SUM_ORDER = [c ^ y ^ z for c in (0, 1) for y in (0, 2, 4, 6) for z in (0, 8, 16, 24)]


def hop(value, mask, axis="tile", size=32):
    return lax.ppermute(value, axis, [(i, i ^ mask) for i in range(size)])


def gather_columns(block):
    held = block[None]
    for masks in (Z_MASKS, Y_MASKS):
        held = jnp.concatenate([held] + [hop(held, m) for m in masks], axis=0)
    return held, hop(held, CORE)


def shifted(value, dr, dc):
    step = ROWS * dc + dr
    moved = pltpu.roll(value, (-step) % POS, 1) if step else value
    if step == 0:
        return moved
    place = lax.broadcasted_iota(jnp.int32, value.shape, 1)
    row, col = place % ROWS + dr, place // ROWS + dc
    inside = (row >= 0) & (row < ROWS) & (col >= 0) & (col < COLS)
    return jnp.where(inside, moved, 0.0)


def assemble(me, near_ref, far_ref, out_ref):
    half = len(ORDER) // 2
    for k, mask in enumerate(ORDER):
        col = me ^ mask
        src = near_ref if k < half else far_ref
        out_ref[pl.ds(pl.multiple_of(col * ROWS, ROWS), ROWS), :] = src[k % half]


def dot(a, b, ca, cb):
    return lax.dot_general(a, b, (((ca,), (cb,)), ((), ())), preferred_element_type=F32)


def forward_kernel(me_ref, near_ref, far_ref, w_ref, gain_ref, bias_ref, x_ref, taps_ref, xhat_ref, slope_ref, rstd_ref):
    assemble(me_ref[0], near_ref, far_ref, x_ref)
    products = dot(w_ref[...], x_ref[...], 1, 1)
    pre = jnp.zeros((OWN, POS), F32)
    for t, (dr, dc) in enumerate(TAPS):
        pre = pre + shifted(products[OWN * t : OWN * (t + 1)], dr, dc)
    count = 1.0 / (OWN * POS)
    mean = jnp.sum(pre, keepdims=True) * count
    centred = pre - mean
    rstd = lax.rsqrt(jnp.sum(centred * centred, keepdims=True) * count + 1e-05)
    xhat = centred * rstd
    normed = xhat * gain_ref[...] + bias_ref[...]
    sig = jax.nn.sigmoid(normed)
    act = (normed * sig).astype(BF).astype(F32)
    for t, (dr, dc) in enumerate(TAPS):
        taps_ref[OWN * t : OWN * (t + 1), :] = shifted(act, dr, dc).astype(BF)
    xhat_ref[...] = xhat
    slope_ref[...] = sig * (1.0 + normed * (1.0 - sig))
    rstd_ref[...] = jnp.broadcast_to(rstd, rstd_ref.shape)


def split_blocks(xi, grad, whole_ref, outs):
    whole_ref[...] = grad
    rows = grad.shape[0]
    for m, out in enumerate(outs):
        lane = pl.multiple_of((xi ^ m) * 256, 256)
        out[:rows, :] = whole_ref[:, pl.ds(lane, 256)].astype(out.dtype)


def second_kernel(me_ref, near_ref, far_ref, taps_ref, dy_ref, g0, g1, g2, g3, whole_ref):
    assemble(me_ref[0], near_ref, far_ref, dy_ref)
    split_blocks(me_ref[1], dot(taps_ref[...], dy_ref[...], 1, 0), whole_ref, (g0, g1, g2, g3))


def turn_kernel(w_ref, out_ref):
    out_ref[:, : 9 * OWN] = w_ref[...].astype(F32).T.astype(BF)
    out_ref[:, 9 * OWN :] = jnp.zeros((CH, 96), BF)


def backward_kernel(
    me_ref, w2_ref, dy_ref, x_ref, w1_ref, gain_ref, xhat_ref, slope_ref, rstd_ref,
    p_near, p_far, g0, g1, g2, g3, w2t_ref, whole_ref, taps_ref, rows_ref,
):
    me = me_ref[0]
    for t in range(9):
        base, at = 128 * (t // 4), OWN * (t % 4)
        for g in range(8):
            parts = [w2_ref[4 * g + j][:, base + at : base + at + OWN].astype(F32) for j in range(4)]
            w2t_ref[OWN * t : OWN * (t + 1), 128 * g : 128 * (g + 1)] = jnp.concatenate(parts, axis=1).astype(BF)
    products = dot(w2t_ref[...], dy_ref[...], 1, 1)
    act_grad = jnp.zeros((OWN, POS), F32)
    for t, (dr, dc) in enumerate(TAPS):
        act_grad = act_grad + shifted(products[OWN * t : OWN * (t + 1)], -dr, -dc)
    xhat = xhat_ref[...]
    norm_grad = act_grad * slope_ref[...]
    gain_sum = jnp.sum(norm_grad * xhat, axis=1, keepdims=True)
    shift_sum = jnp.sum(norm_grad, axis=1, keepdims=True)
    scaled = norm_grad * gain_ref[...]
    count = 1.0 / (OWN * POS)
    first_mean = jnp.sum(scaled, keepdims=True) * count
    second_mean = jnp.sum(scaled * xhat, keepdims=True) * count
    pre_grad = rstd_ref[0:1, 0:1] * (scaled - first_mean - xhat * second_mean)
    pre_grad = pre_grad.astype(BF).astype(F32)
    for t, (dr, dc) in enumerate(TAPS):
        taps_ref[OWN * t : OWN * (t + 1), :] = shifted(pre_grad, -dr, -dc)
    taps = taps_ref[...]
    split_blocks(me_ref[1], dot(taps.astype(BF), x_ref[...], 1, 0), whole_ref, (g0, g1, g2, g3))
    high_g = gain_sum.astype(BF).astype(F32)
    high_s = shift_sum.astype(BF).astype(F32)
    lane = lax.broadcasted_iota(jnp.int32, (OWN, 128), 1)
    sums = jnp.where(lane == 0, high_g, 0.0) + jnp.where(lane == 1, gain_sum - high_g, 0.0)
    sums = sums + jnp.where(lane == 2, high_s, 0.0) + jnp.where(lane == 3, shift_sum - high_s, 0.0)
    extra = sums.T[:16, :]
    for out in (g0, g1, g2, g3):
        out[9 * OWN :, :] = jnp.zeros((16, 256), out.dtype)
        out[9 * OWN :, :OWN] = extra.astype(out.dtype)
    rows_ref[...] = taps.T
    half = len(SUM_ORDER) // 2
    for part, out in enumerate((p_near, p_far)):
        blocks = []
        for mask in SUM_ORDER[part * half : (part + 1) * half]:
            start = pl.multiple_of((me ^ mask) * ROWS, ROWS)
            blocks.append(rows_ref[pl.ds(start, ROWS), :])
        out[...] = dot(jnp.concatenate(blocks, axis=0).astype(BF), w1_ref[...], 1, 0)


def finish_kernel(me_ref, a0, a1, a2, a3, out_ref):
    for m, part in enumerate((a0, a1, a2, a3)):
        lane = pl.multiple_of((me_ref[1] ^ m) * 256, 256)
        out_ref[:, pl.ds(lane, 256)] = part[: 9 * OWN, :].astype(F32)


def call(kernel, outs, scratch=(), n_in=1, flops=0):
    smem = pl.BlockSpec(memory_space=pltpu.SMEM)
    vmem = pl.BlockSpec(memory_space=pltpu.VMEM)
    return pl.pallas_call(
        kernel,
        out_shape=[jax.ShapeDtypeStruct(s, d) for s, d in outs],
        in_specs=[smem] + [vmem] * n_in,
        out_specs=[vmem] * len(outs),
        scratch_shapes=[pltpu.VMEM(s, d) for s, d in scratch],
        compiler_params=pltpu.CompilerParams(vmem_limit_bytes=32 * MB),
        cost_estimate=pl.CostEstimate(flops=flops, bytes_accessed=4 * MB, transcendentals=0),
    )


def sum_over_sample(parts):
    total = parts[0]
    got = [hop(parts[m], 2 * m, "sample", 8) for m in (1, 2, 3)]
    for r in got:
        total = total + r.astype(F32)
    mine = total.astype(BF)
    mine = (mine.astype(F32) + hop(mine, 1, "sample", 8).astype(F32)).astype(BF)
    return [mine] + [hop(mine, 2 * m, "sample", 8) for m in (1, 2, 3)]


def per_device(inputs, first_weight, second_weight, norm_gain_vector, norm_bias, cotangent):
    tile = lax.axis_index("tile").astype(jnp.int32)
    place = jnp.stack([tile, (lax.axis_index("sample") // 2).astype(jnp.int32)])
    x_near, x_far = gather_columns(inputs.reshape(ROWS, CH))
    dy_near, dy_far = gather_columns(cotangent.reshape(ROWS, CH))
    w1 = first_weight.reshape(9 * OWN, CH)
    w2 = second_weight.reshape(9 * OWN, CH)
    gain, bias = norm_gain_vector[:, None], norm_bias[:, None]
    vmem = pl.BlockSpec(memory_space=pltpu.VMEM)
    turned = pl.pallas_call(
        turn_kernel,
        out_shape=jax.ShapeDtypeStruct((CH, 384), BF),
        in_specs=[vmem],
        out_specs=vmem,
        compiler_params=pltpu.CompilerParams(vmem_limit_bytes=32 * MB),
    )(w2)
    w2_own = lax.all_to_all(turned.reshape(32, OWN, 384), "tile", split_axis=0, concat_axis=0, tiled=True)
    flops = 2 * 288 * POS * CH
    x_all, act_taps, xhat, slope, rstd = call(
        forward_kernel,
        [((POS, CH), BF), ((9 * OWN, POS), BF), ((OWN, POS), F32), ((OWN, POS), F32), ((8, 128), F32)],
        n_in=5, flops=flops,
    )(place, x_near, x_far, w1, gain, bias)
    blocks = [((9 * OWN, 256), F32)] + [((9 * OWN, 256), BF)] * 3
    whole = [((9 * OWN, CH), F32)]
    dy_all, *second_parts = call(second_kernel, [((POS, CH), BF)] + blocks, whole, n_in=3, flops=flops)(
        place, dy_near, dy_far, act_taps
    )
    blocks = [((9 * OWN + 16, 256), F32)] + [((9 * OWN + 16, 256), BF)] * 3
    near, far, *first_parts = call(
        backward_kernel,
        [((POS // 2, CH), F32)] * 2 + blocks,
        [((9 * OWN, CH), BF)] + whole + [((9 * OWN, POS), F32), ((POS, 9 * OWN), F32)],
        n_in=8, flops=3 * flops,
    )(place, w2_own, dy_all, x_all, w1, gain, xhat, slope, rstd)
    total = (near + hop(far, CORE)).reshape(4, POS // 8, CH)
    got = [hop(total[k].astype(BF), m) for k, m in zip((1, 2, 3), Y_MASKS)]
    total = total[0] + got[0].astype(F32) + got[1].astype(F32) + got[2].astype(F32)
    total = total.reshape(4, ROWS, CH)
    got = [hop(total[k], m) for k, m in zip((1, 2, 3), Z_MASKS)]
    total = total[0] + got[0] + got[1] + got[2]
    conv_back = total.astype(BF).astype(F32)
    input_grad = (cotangent.reshape(ROWS, CH).astype(F32) + conv_back).astype(BF)
    second = sum_over_sample(second_parts)
    first = sum_over_sample(first_parts)
    (second_grad,) = call(finish_kernel, [((9 * OWN, CH), F32)], n_in=4)(place, *second)
    (first_grad,) = call(finish_kernel, [((9 * OWN, CH), F32)], n_in=4)(place, *first)
    xi = place[1]
    extras = jnp.stack([p[9 * OWN : 9 * OWN + 4, :OWN] for p in first]).astype(F32)
    sums = lax.dynamic_index_in_dim(extras, xi, 0, keepdims=False)
    return (
        input_grad.reshape(1, ROWS, 1, CH),
        first_grad.reshape(9, OWN, CH),
        jnp.transpose(second_grad.reshape(9, OWN, CH), (0, 2, 1)),
        sums[0] + sums[1],
        sums[2] + sums[3],
    )


def solution(mesh):
    return jax.shard_map(
        per_device,
        mesh=mesh,
        in_specs=(
            P("sample", None, "tile", None),
            P(None, "tile", None),
            P(None, "tile", None),
            P("tile"),
            P("tile"),
            P("sample", None, "tile", None),
        ),
        out_specs=(
            P("sample", None, "tile", None),
            P(None, "tile", None),
            P(None, None, "tile"),
            P("tile"),
            P("tile"),
        ),
        check_vma=False,
    )
```

```python
import functools

import jax
import jax.numpy as jnp
from jax import lax
from jax.experimental import pallas as pl
from jax.experimental.pallas import tpu as pltpu
from jax.sharding import PartitionSpec as P

BF = jnp.bfloat16
F32 = jnp.float32
TAPS = [(dr, dc) for dr in (-1, 0, 1) for dc in (-1, 0, 1)]
ROWS, COLS, CH = 16, 32, 1024
POS = ROWS * COLS
OWN = 32
MB = 1 << 20

Z_MASKS, Y_MASKS, CORE = (8, 16, 24), (2, 4, 6), 1
ORDER = [c ^ y ^ z for c in (0, 1) for y in (0, 2, 4, 6) for z in (0, 8, 16, 24)]
SUM_ORDER = [c ^ y ^ z for c in (0, 1) for y in (0, 2, 4, 6) for z in (0, 8, 16, 24)]


def hop(value, mask, axis="tile", size=32):
    return lax.ppermute(value, axis, [(i, i ^ mask) for i in range(size)])


def shifted(value, dr, dc):
    step = ROWS * dc + dr
    moved = pltpu.roll(value, (-step) % POS, 1) if step else value
    if step == 0:
        return moved
    place = lax.broadcasted_iota(jnp.int32, value.shape, 1)
    row, col = place % ROWS + dr, place // ROWS + dc
    inside = (row >= 0) & (row < ROWS) & (col >= 0) & (col < COLS)
    return jnp.where(inside, moved, 0.0)


def assemble(me, near_ref, far_ref, out_ref, at):
    half = len(ORDER) // 2
    for k, mask in enumerate(ORDER):
        src = near_ref if k < half else far_ref
        out_ref[me ^ mask] = src[k % half, at : at + ROWS, :]


def x_index():
    return lax.axis_index("sample") // 2


def column(row):
    i = lax.broadcasted_iota(jnp.int32, (OWN, OWN), 0)
    j = lax.broadcasted_iota(jnp.int32, (OWN, OWN), 1)
    return jnp.sum(jnp.where(i == j, jnp.broadcast_to(row, (OWN, OWN)), 0.0), axis=1, keepdims=True)


def dot(a, b, ca, cb):
    return lax.dot_general(a, b, (((ca,), (cb,)), ((), ())), preferred_element_type=F32)


def main_kernel(
    near_ref, far_ref, w2_ref, w1_ref, gain_ref, bias_ref,
    p_near, p_far, g0, g1, g2, g3,
    x_ref, dy_ref, act_ref, w2t_ref, taps_ref, rows_ref, whole_ref,
):
    me = lax.axis_index("tile")
    assemble(me, near_ref, far_ref, x_ref, 0)
    products = dot(w1_ref[...], x_ref[...].reshape(POS, CH), 1, 1)
    pre = jnp.zeros((OWN, POS), F32)
    for t, (dr, dc) in enumerate(TAPS):
        pre = pre + shifted(products[OWN * t : OWN * (t + 1)], dr, dc)
    count = 1.0 / (OWN * POS)
    mean = jnp.sum(pre, keepdims=True) * count
    centred = pre - mean
    rstd = lax.rsqrt(jnp.sum(centred * centred, keepdims=True) * count + 1e-05)
    xhat = centred * rstd
    gain = column(gain_ref[...])
    normed = xhat * gain + column(bias_ref[...])
    sig = jax.nn.sigmoid(normed)
    act = (normed * sig).astype(BF).astype(F32)
    for t, (dr, dc) in enumerate(TAPS):
        act_ref[OWN * t : OWN * (t + 1), :] = shifted(act, dr, dc).astype(BF)
    slope = sig * (1.0 + normed * (1.0 - sig))
    assemble(me, near_ref, far_ref, dy_ref, ROWS)
    xi = x_index()
    outs = (g0, g1, g2, g3)
    grad = dot(act_ref[...], dy_ref[...].reshape(POS, CH), 1, 0)
    split_blocks(xi, grad, whole_ref, outs, 9 * OWN + 16)
    for g in range(8):
        lanes = slice(128 * g, 128 * (g + 1))
        for t in range(8):
            rows, at = slice(OWN * (t // 4), OWN * (t // 4 + 1)), OWN * (t % 4)
            parts = [w2_ref[4 * g + j, rows, at : at + OWN].astype(F32) for j in range(4)]
            w2t_ref[OWN * t : OWN * (t + 1), lanes] = jnp.concatenate(parts, axis=1).astype(BF)
        tails = [w2_ref[4 * g + j, 2 * OWN :, :].astype(F32)[:8] for j in range(4)]
        parts = [jnp.concatenate([v[:, OWN * a : OWN * (a + 1)] for v in tails], axis=1) for a in range(4)]
        w2t_ref[8 * OWN :, lanes] = jnp.concatenate(parts, axis=0).astype(BF)
    products = dot(w2t_ref[...], dy_ref[...].reshape(POS, CH), 1, 1)
    act_grad = jnp.zeros((OWN, POS), F32)
    for t, (dr, dc) in enumerate(TAPS):
        act_grad = act_grad + shifted(products[OWN * t : OWN * (t + 1)], -dr, -dc)
    norm_grad = act_grad * slope
    gain_sum = jnp.sum(norm_grad * xhat, axis=1, keepdims=True)
    shift_sum = jnp.sum(norm_grad, axis=1, keepdims=True)
    scaled = norm_grad * gain
    count = 1.0 / (OWN * POS)
    first_mean = jnp.sum(scaled, keepdims=True) * count
    second_mean = jnp.sum(scaled * xhat, keepdims=True) * count
    pre_grad = rstd * (scaled - first_mean - xhat * second_mean)
    pre_grad = pre_grad.astype(BF).astype(F32)
    for t, (dr, dc) in enumerate(TAPS):
        taps_ref[OWN * t : OWN * (t + 1), :] = shifted(pre_grad, -dr, -dc)
    taps = taps_ref[...]
    grad = dot(taps.astype(BF), x_ref[...].reshape(POS, CH), 1, 0)
    split_blocks(xi, grad, whole_ref, outs, 0)
    high_g = gain_sum.astype(BF).astype(F32)
    high_s = shift_sum.astype(BF).astype(F32)
    lane = lax.broadcasted_iota(jnp.int32, (OWN, 128), 1)
    sums = jnp.where(lane == 0, high_g, 0.0) + jnp.where(lane == 1, gain_sum - high_g, 0.0)
    sums = sums + jnp.where(lane == 2, high_s, 0.0) + jnp.where(lane == 3, shift_sum - high_s, 0.0)
    extra = sums.T[:16, :]
    rows = slice(9 * OWN, 9 * OWN + 16)
    for out in outs:
        out[rows, :] = jnp.zeros((16, 256), out.dtype)
        out[rows, :OWN] = extra.astype(out.dtype)
    rows_ref[...] = taps.T
    half = len(SUM_ORDER) // 2
    for part, out in enumerate((p_near, p_far)):
        blocks = []
        for mask in SUM_ORDER[part * half : (part + 1) * half]:
            start = pl.multiple_of((me ^ mask) * ROWS, ROWS)
            blocks.append(rows_ref[pl.ds(start, ROWS), :])
        out[...] = dot(jnp.concatenate(blocks, axis=0).astype(BF), w1_ref[...], 1, 0)


def split_blocks(xi, grad, whole_ref, outs, at):
    whole_ref[...] = grad
    rows = slice(at, at + grad.shape[0])
    for m, out in enumerate(outs):
        lane = pl.multiple_of((xi ^ m) * 256, 256)
        out[rows, :] = whole_ref[:, pl.ds(lane, 256)].astype(out.dtype)


def turn_kernel(w_ref, out_ref):
    turned = w_ref[...].astype(F32).T
    out_ref[:, :OWN, :] = turned[:, :128].reshape(32, OWN, 128).astype(BF)
    out_ref[:, OWN : 2 * OWN, :] = turned[:, 128:256].reshape(32, OWN, 128).astype(BF)
    last = turned[:, 256:].reshape(32, 4, 8, OWN)
    last = jnp.concatenate([last[:, a] for a in range(4)], axis=2)
    out_ref[:, 2 * OWN :, :] = jnp.concatenate([last, jnp.zeros_like(last)], axis=1).astype(BF)


def finish_kernel(a0, a1, a2, a3, first_ref, second_ref, gain_ref, shift_ref):
    xi = x_index()
    sums = jnp.zeros((16, 256), F32)
    for m, part in enumerate((a0, a1, a2, a3)):
        lanes = pl.ds(pl.multiple_of((xi ^ m) * 256, 256), 256)
        first_ref[:, lanes] = part[: 9 * OWN, :].astype(F32)
        second_ref[:, lanes] = part[9 * OWN + 16 :, :].astype(F32)
        sums = jnp.where(xi == m, part[9 * OWN : 9 * OWN + 16, :].astype(F32), sums)
    gain_ref[...] = sums[0:1, :OWN] + sums[1:2, :OWN]
    shift_ref[...] = sums[2:3, :OWN] + sums[3:4, :OWN]


LIMIT = 14 * MB


def call(kernel, operands, outs, scratch=(), flops=0):
    vmem = pl.BlockSpec(memory_space=pltpu.VMEM)
    return pl.pallas_call(
        kernel,
        out_shape=[jax.ShapeDtypeStruct(s, d) for s, d in outs],
        in_specs=[vmem] * len(operands),
        out_specs=[vmem] * len(outs),
        scratch_shapes=[pltpu.VMEM(s, d) for s, d in scratch],
        compiler_params=pltpu.CompilerParams(vmem_limit_bytes=LIMIT),
        cost_estimate=pl.CostEstimate(flops=flops, bytes_accessed=4 * MB, transcendentals=0),
    )(*operands)


def resplit(total):
    gain = total[9 * OWN : 9 * OWN + 1] + total[9 * OWN + 1 : 9 * OWN + 2]
    shift = total[9 * OWN + 2 : 9 * OWN + 3] + total[9 * OWN + 3 : 9 * OWN + 4]
    high_g, high_s = gain.astype(BF).astype(F32), shift.astype(BF).astype(F32)
    row = lax.broadcasted_iota(jnp.int32, (16, 256), 0)
    extra = jnp.where(row == 0, high_g, 0.0) + jnp.where(row == 1, gain - high_g, 0.0)
    extra = extra + jnp.where(row == 2, high_s, 0.0) + jnp.where(row == 3, shift - high_s, 0.0)
    return extra.astype(BF)


def x_sum_kernel(own_ref, r1, r2, r3, out_ref):
    total = own_ref[...] + r1[...].astype(F32) + r2[...].astype(F32) + r3[...].astype(F32)
    out_ref[...] = total.astype(BF)
    out_ref[9 * OWN : 9 * OWN + 16, :] = resplit(total)


def z_sum_kernel(mine_ref, other_ref, out_ref):
    total = mine_ref[...].astype(F32) + other_ref[...].astype(F32)
    out_ref[...] = total.astype(BF)
    out_ref[9 * OWN : 9 * OWN + 16, :] = resplit(total)


def x_hops(parts):
    return [parts[0]] + [hop(parts[m], 2 * m, "sample", 8) for m in (1, 2, 3)]


def z_hop(mine):
    return hop(mine, 1, "sample", 8)


def spread(mine):
    return [mine] + [hop(mine, 2 * m, "sample", 8) for m in (1, 2, 3)]


def after(value, *others):
    return lax.optimization_barrier((value, *others))[0]


def per_device(inputs, first_weight, second_weight, norm_gain_vector, norm_bias, cotangent):
    w2 = second_weight.reshape(9 * OWN, CH)
    (turned,) = call(turn_kernel, [w2], [((32, 80, 128), BF)])
    block = jnp.concatenate([inputs.reshape(1, ROWS, CH), cotangent.reshape(1, ROWS, CH)], axis=1)
    held = jnp.concatenate([block] + [hop(block, m) for m in Z_MASKS])
    got = [hop(held, m) for m in Y_MASKS]
    w2_own = lax.all_to_all(turned, "tile", split_axis=0, concat_axis=0, tiled=True)
    near = jnp.concatenate([held] + got)
    far = hop(near, CORE)
    w1 = first_weight.reshape(9 * OWN, CH)
    gain, bias = norm_gain_vector.reshape(1, OWN), norm_bias.reshape(1, OWN)
    flops = 2 * 288 * POS * CH
    columns, taps, whole = (COLS, ROWS, CH), (9 * OWN, POS), (9 * OWN, CH)
    joint = (18 * OWN + 16, 256)
    conv_near, conv_far, *parts = call(
        main_kernel,
        [near, far, w2_own, w1, gain, bias],
        [((POS // 2, CH), F32)] * 2 + [(joint, F32)] + [(joint, BF)] * 3,
        [(columns, BF), (columns, BF), (taps, BF), (whole, BF), (taps, F32), ((POS, 9 * OWN), F32), (whole, F32)],
        5 * flops,
    )
    conv_far = hop(conv_far, CORE)
    parts = x_hops(parts)
    (mine,) = call(x_sum_kernel, parts, [(joint, BF)])
    other = z_hop(mine)
    total = after((conv_near + conv_far).reshape(4, POS // 8, CH), *parts[1:])
    got = [hop(total[k].astype(BF), m) for k, m in zip((1, 2, 3), Y_MASKS)]
    total = total[0] + got[0].astype(F32) + got[1].astype(F32) + got[2].astype(F32)
    total = total.reshape(4, ROWS, CH)
    (summed,) = call(z_sum_kernel, [mine, other], [(joint, BF)])
    blocks = spread(after(summed, total))
    got = [hop(total[k], m) for k, m in zip((1, 2, 3), Z_MASKS)]
    total = total[0] + got[0] + got[1] + got[2]
    conv_back = total.astype(BF).astype(F32)
    input_grad = (cotangent.reshape(ROWS, CH).astype(F32) + conv_back).astype(BF)
    grad, row = ((9 * OWN, CH), F32), ((1, OWN), F32)
    first_grad, second_grad, gain_grad, shift_grad = call(finish_kernel, blocks, [grad, grad, row, row])
    return (
        input_grad.reshape(1, ROWS, 1, CH),
        first_grad.reshape(9, OWN, CH),
        jnp.transpose(second_grad.reshape(9, OWN, CH), (0, 2, 1)),
        gain_grad.reshape(OWN),
        shift_grad.reshape(OWN),
    )


def solution(mesh):
    return jax.shard_map(
        per_device,
        mesh=mesh,
        in_specs=(
            P("sample", None, "tile", None),
            P(None, "tile", None),
            P(None, "tile", None),
            P("tile"),
            P("tile"),
            P("sample", None, "tile", None),
        ),
        out_specs=(
            P("sample", None, "tile", None),
            P(None, "tile", None),
            P(None, None, "tile"),
            P("tile"),
            P("tile"),
        ),
        check_vma=False,
    )
```

```python
import functools

import jax
import jax.numpy as jnp
from jax import lax
from jax.experimental import pallas as pl
from jax.experimental.pallas import tpu as pltpu
from jax.sharding import PartitionSpec as P

BF = jnp.bfloat16
F32 = jnp.float32
TAPS = [(dr, dc) for dr in (-1, 0, 1) for dc in (-1, 0, 1)]
ROWS, COLS, CH = 16, 32, 1024
POS = ROWS * COLS
OWN = 32
MB = 1 << 20

Z_MASKS, Y_MASKS, CORE = (8, 16, 24), (2, 4, 6), 1
ORDER = [c ^ y ^ z for c in (0, 1) for y in (0, 2, 4, 6) for z in (0, 8, 16, 24)]
SUM_ORDER = [c ^ y ^ z for c in (0, 1) for y in (0, 2, 4, 6) for z in (0, 8, 16, 24)]


def hop(value, mask, axis="tile", size=32):
    return lax.ppermute(value, axis, [(i, i ^ mask) for i in range(size)])


def shifted(value, dr, dc):
    step = ROWS * dc + dr
    moved = pltpu.roll(value, (-step) % POS, 1) if step else value
    if step == 0:
        return moved
    place = lax.broadcasted_iota(jnp.int32, value.shape, 1)
    row, col = place % ROWS + dr, place // ROWS + dc
    inside = (row >= 0) & (row < ROWS) & (col >= 0) & (col < COLS)
    return jnp.where(inside, moved, 0.0)


def assemble(me, near_ref, far_ref, out_ref, at):
    half = len(ORDER) // 2
    for k, mask in enumerate(ORDER):
        src = near_ref if k < half else far_ref
        out_ref[me ^ mask] = src[k % half, at : at + ROWS, :]


def x_index():
    return lax.axis_index("sample") // 2


def column(row):
    i = lax.broadcasted_iota(jnp.int32, (OWN, OWN), 0)
    j = lax.broadcasted_iota(jnp.int32, (OWN, OWN), 1)
    return jnp.sum(jnp.where(i == j, jnp.broadcast_to(row, (OWN, OWN)), 0.0), axis=1, keepdims=True)


def dot(a, b, ca, cb):
    return lax.dot_general(a, b, (((ca,), (cb,)), ((), ())), preferred_element_type=F32)


def main_kernel(
    near_ref, far_ref, w2_ref, w1_ref, gain_ref, bias_ref,
    p_near, p_far, g0, g1, g2, g3,
    x_ref, dy_ref, act_ref, w2t_ref, taps_ref, rows_ref, whole_ref,
):
    me = lax.axis_index("tile")
    assemble(me, near_ref, far_ref, x_ref, 0)
    products = dot(w1_ref[...], x_ref[...].reshape(POS, CH), 1, 1)
    pre = jnp.zeros((OWN, POS), F32)
    for t, (dr, dc) in enumerate(TAPS):
        pre = pre + shifted(products[OWN * t : OWN * (t + 1)], dr, dc)
    count = 1.0 / (OWN * POS)
    mean = jnp.sum(pre, keepdims=True) * count
    centred = pre - mean
    rstd = lax.rsqrt(jnp.sum(centred * centred, keepdims=True) * count + 1e-05)
    xhat = centred * rstd
    gain = column(gain_ref[...])
    normed = xhat * gain + column(bias_ref[...])
    sig = jax.nn.sigmoid(normed)
    act = (normed * sig).astype(BF).astype(F32)
    for t, (dr, dc) in enumerate(TAPS):
        act_ref[OWN * t : OWN * (t + 1), :] = shifted(act, dr, dc).astype(BF)
    slope = sig * (1.0 + normed * (1.0 - sig))
    assemble(me, near_ref, far_ref, dy_ref, ROWS)
    xi = x_index()
    outs = (g0, g1, g2, g3)
    grad = dot(act_ref[...], dy_ref[...].reshape(POS, CH), 1, 0)
    split_blocks(xi, grad, whole_ref, outs, 9 * OWN + 16)
    for g in range(8):
        lanes = slice(128 * g, 128 * (g + 1))
        for t in range(8):
            rows, at = slice(OWN * (t // 4), OWN * (t // 4 + 1)), OWN * (t % 4)
            parts = [w2_ref[4 * g + j, rows, at : at + OWN].astype(F32) for j in range(4)]
            w2t_ref[OWN * t : OWN * (t + 1), lanes] = jnp.concatenate(parts, axis=1).astype(BF)
        tails = [w2_ref[4 * g + j, 2 * OWN :, :].astype(F32)[:8] for j in range(4)]
        parts = [jnp.concatenate([v[:, OWN * a : OWN * (a + 1)] for v in tails], axis=1) for a in range(4)]
        w2t_ref[8 * OWN :, lanes] = jnp.concatenate(parts, axis=0).astype(BF)
    products = dot(w2t_ref[...], dy_ref[...].reshape(POS, CH), 1, 1)
    act_grad = jnp.zeros((OWN, POS), F32)
    for t, (dr, dc) in enumerate(TAPS):
        act_grad = act_grad + shifted(products[OWN * t : OWN * (t + 1)], -dr, -dc)
    norm_grad = act_grad * slope
    gain_sum = jnp.sum(norm_grad * xhat, axis=1, keepdims=True)
    shift_sum = jnp.sum(norm_grad, axis=1, keepdims=True)
    scaled = norm_grad * gain
    count = 1.0 / (OWN * POS)
    first_mean = jnp.sum(scaled, keepdims=True) * count
    second_mean = jnp.sum(scaled * xhat, keepdims=True) * count
    pre_grad = rstd * (scaled - first_mean - xhat * second_mean)
    pre_grad = pre_grad.astype(BF).astype(F32)
    for t, (dr, dc) in enumerate(TAPS):
        taps_ref[OWN * t : OWN * (t + 1), :] = shifted(pre_grad, -dr, -dc)
    taps = taps_ref[...]
    grad = dot(taps.astype(BF), x_ref[...].reshape(POS, CH), 1, 0)
    split_blocks(xi, grad, whole_ref, outs, 0)
    high_g = gain_sum.astype(BF).astype(F32)
    high_s = shift_sum.astype(BF).astype(F32)
    lane = lax.broadcasted_iota(jnp.int32, (OWN, 128), 1)
    sums = jnp.where(lane == 0, high_g, 0.0) + jnp.where(lane == 1, gain_sum - high_g, 0.0)
    sums = sums + jnp.where(lane == 2, high_s, 0.0) + jnp.where(lane == 3, shift_sum - high_s, 0.0)
    extra = sums.T[:16, :]
    rows = slice(9 * OWN, 9 * OWN + 16)
    for out in outs:
        out[rows, :] = jnp.zeros((16, 256), out.dtype)
        out[rows, :OWN] = extra.astype(out.dtype)
    rows_ref[...] = taps.T
    half = len(SUM_ORDER) // 2
    for part, out in enumerate((p_near, p_far)):
        blocks = []
        for mask in SUM_ORDER[part * half : (part + 1) * half]:
            start = pl.multiple_of((me ^ mask) * ROWS, ROWS)
            blocks.append(rows_ref[pl.ds(start, ROWS), :])
        out[...] = dot(jnp.concatenate(blocks, axis=0).astype(BF), w1_ref[...], 1, 0)


def split_blocks(xi, grad, whole_ref, outs, at):
    whole_ref[...] = grad
    rows = slice(at, at + grad.shape[0])
    for m, out in enumerate(outs):
        lane = pl.multiple_of((xi ^ m) * 256, 256)
        out[rows, :] = whole_ref[:, pl.ds(lane, 256)].astype(out.dtype)


def turn_kernel(w_ref, out_ref):
    turned = w_ref[...].astype(F32).T
    out_ref[:, :OWN, :] = turned[:, :128].reshape(32, OWN, 128).astype(BF)
    out_ref[:, OWN : 2 * OWN, :] = turned[:, 128:256].reshape(32, OWN, 128).astype(BF)
    last = turned[:, 256:].reshape(32, 4, 8, OWN)
    last = jnp.concatenate([last[:, a] for a in range(4)], axis=2)
    out_ref[:, 2 * OWN :, :] = jnp.concatenate([last, jnp.zeros_like(last)], axis=1).astype(BF)


def finish_kernel(a0, a1, a2, a3, first_ref, second_ref, gain_ref, shift_ref):
    xi = x_index()
    sums = jnp.zeros((16, 256), F32)
    for m, part in enumerate((a0, a1, a2, a3)):
        lanes = pl.ds(pl.multiple_of((xi ^ m) * 256, 256), 256)
        first_ref[:, lanes] = part[: 9 * OWN, :].astype(F32)
        second_ref[:, lanes] = part[9 * OWN + 16 :, :].astype(F32)
        sums = jnp.where(xi == m, part[9 * OWN : 9 * OWN + 16, :].astype(F32), sums)
    gain_ref[...] = sums[0:1, :OWN] + sums[1:2, :OWN]
    shift_ref[...] = sums[2:3, :OWN] + sums[3:4, :OWN]


LIMIT = 14 * MB


def call(kernel, operands, outs, scratch=(), flops=0):
    vmem = pl.BlockSpec(memory_space=pltpu.VMEM)
    return pl.pallas_call(
        kernel,
        out_shape=[jax.ShapeDtypeStruct(s, d) for s, d in outs],
        in_specs=[vmem] * len(operands),
        out_specs=[vmem] * len(outs),
        scratch_shapes=[pltpu.VMEM(s, d) for s, d in scratch],
        compiler_params=pltpu.CompilerParams(vmem_limit_bytes=LIMIT),
        cost_estimate=pl.CostEstimate(flops=flops, bytes_accessed=4 * MB, transcendentals=0),
    )(*operands)


def resplit(total):
    gain = total[9 * OWN : 9 * OWN + 1] + total[9 * OWN + 1 : 9 * OWN + 2]
    shift = total[9 * OWN + 2 : 9 * OWN + 3] + total[9 * OWN + 3 : 9 * OWN + 4]
    high_g, high_s = gain.astype(BF).astype(F32), shift.astype(BF).astype(F32)
    row = lax.broadcasted_iota(jnp.int32, (16, 256), 0)
    extra = jnp.where(row == 0, high_g, 0.0) + jnp.where(row == 1, gain - high_g, 0.0)
    extra = extra + jnp.where(row == 2, high_s, 0.0) + jnp.where(row == 3, shift - high_s, 0.0)
    return extra.astype(BF)


def x_sum_kernel(own_ref, r1, r2, r3, out_ref):
    total = own_ref[...] + r1[...].astype(F32) + r2[...].astype(F32) + r3[...].astype(F32)
    out_ref[...] = total.astype(BF)
    out_ref[9 * OWN : 9 * OWN + 16, :] = resplit(total)


def z_sum_kernel(mine_ref, other_ref, out_ref):
    total = mine_ref[...].astype(F32) + other_ref[...].astype(F32)
    out_ref[...] = total.astype(BF)
    out_ref[9 * OWN : 9 * OWN + 16, :] = resplit(total)


def x_hops(parts):
    return [parts[0]] + [hop(parts[m], 2 * m, "sample", 8) for m in (1, 2, 3)]


def z_hop(mine):
    return hop(mine, 1, "sample", 8)


def spread(mine):
    return [mine] + [hop(mine, 2 * m, "sample", 8) for m in (1, 2, 3)]


def after(value, *others):
    return lax.optimization_barrier((value, *others))[0]


def per_device(inputs, first_weight, second_weight, norm_gain_vector, norm_bias, cotangent):
    w2 = second_weight.reshape(9 * OWN, CH)
    (turned,) = call(turn_kernel, [w2], [((32, 80, 128), BF)])
    block = jnp.concatenate([inputs.reshape(1, ROWS, CH), cotangent.reshape(1, ROWS, CH)], axis=1)
    held = jnp.concatenate([block] + [hop(block, m) for m in Z_MASKS])
    got = [hop(held, m) for m in Y_MASKS]
    w2_own = lax.all_to_all(turned, "tile", split_axis=0, concat_axis=0, tiled=True)
    near = jnp.concatenate([held] + got)
    far = hop(near, CORE)
    w1 = first_weight.reshape(9 * OWN, CH)
    gain, bias = norm_gain_vector.reshape(1, OWN), norm_bias.reshape(1, OWN)
    flops = 2 * 288 * POS * CH
    columns, taps, whole = (COLS, ROWS, CH), (9 * OWN, POS), (9 * OWN, CH)
    joint = (18 * OWN + 16, 256)
    conv_near, conv_far, *parts = call(
        main_kernel,
        [near, far, w2_own, w1, gain, bias],
        [((POS // 2, CH), F32)] * 2 + [(joint, F32)] + [(joint, BF)] * 3,
        [(columns, BF), (columns, BF), (taps, BF), (whole, BF), (taps, F32), ((POS, 9 * OWN), F32), (whole, F32)],
        5 * flops,
    )
    parts = x_hops(parts)
    conv_far = hop(conv_far, CORE)
    total = (conv_near + conv_far).reshape(4, POS // 8, CH)
    y_got = [hop(total[k].astype(BF), m) for k, m in zip((1, 2, 3), Y_MASKS)]
    (mine,) = call(x_sum_kernel, [after(parts[0], *y_got), *parts[1:]], [(joint, BF)])
    other = z_hop(mine)
    total = total[0] + y_got[0].astype(F32) + y_got[1].astype(F32) + y_got[2].astype(F32)
    total = after(total.reshape(4, ROWS, CH), other)
    z_got = [hop(total[k].astype(BF), m) for k, m in zip((1, 2, 3), Z_MASKS)]
    (summed,) = call(z_sum_kernel, [mine, other], [(joint, BF)])
    blocks = spread(summed)
    total = total[0] + z_got[0].astype(F32) + z_got[1].astype(F32) + z_got[2].astype(F32)
    conv_back = total.astype(BF).astype(F32)
    input_grad = (cotangent.reshape(ROWS, CH).astype(F32) + conv_back).astype(BF)
    grad, row = ((9 * OWN, CH), F32), ((1, OWN), F32)
    first_grad, second_grad, gain_grad, shift_grad = call(finish_kernel, blocks, [grad, grad, row, row])
    return (
        input_grad.reshape(1, ROWS, 1, CH),
        first_grad.reshape(9, OWN, CH),
        jnp.transpose(second_grad.reshape(9, OWN, CH), (0, 2, 1)),
        gain_grad.reshape(OWN),
        shift_grad.reshape(OWN),
    )


def solution(mesh):
    return jax.shard_map(
        per_device,
        mesh=mesh,
        in_specs=(
            P("sample", None, "tile", None),
            P(None, "tile", None),
            P(None, "tile", None),
            P("tile"),
            P("tile"),
            P("sample", None, "tile", None),
        ),
        out_specs=(
            P("sample", None, "tile", None),
            P(None, "tile", None),
            P(None, None, "tile"),
            P("tile"),
            P("tile"),
        ),
        check_vma=False,
    )
```

```python
import functools

import jax
import jax.numpy as jnp
from jax import lax
from jax.experimental import pallas as pl
from jax.experimental.pallas import tpu as pltpu
from jax.sharding import PartitionSpec as P

BF = jnp.bfloat16
F32 = jnp.float32
TAPS = [(dr, dc) for dr in (-1, 0, 1) for dc in (-1, 0, 1)]
ROWS, COLS, CH = 16, 32, 1024
POS = ROWS * COLS
OWN = 32
MB = 1 << 20

Z_MASKS, Y_MASKS, CORE = (8, 16, 24), (2, 4, 6), 1
ORDER = [c ^ y ^ z for c in (0, 1) for y in (0, 2, 4, 6) for z in (0, 8, 16, 24)]
SUM_ORDER = [c ^ y ^ z for c in (0, 1) for y in (0, 2, 4, 6) for z in (0, 8, 16, 24)]


def hop(value, mask, axis="tile", size=32):
    return lax.ppermute(value, axis, [(i, i ^ mask) for i in range(size)])


def shifted(value, dr, dc):
    step = ROWS * dc + dr
    moved = pltpu.roll(value, (-step) % POS, 1) if step else value
    if step == 0:
        return moved
    place = lax.broadcasted_iota(jnp.int32, value.shape, 1)
    row, col = place % ROWS + dr, place // ROWS + dc
    inside = (row >= 0) & (row < ROWS) & (col >= 0) & (col < COLS)
    return jnp.where(inside, moved, 0.0)


def assemble(me, near_ref, far_ref, out_ref, at):
    half = len(ORDER) // 2
    for k, mask in enumerate(ORDER):
        src = near_ref if k < half else far_ref
        out_ref[me ^ mask] = src[k % half, at : at + ROWS, :]


def x_index():
    return lax.axis_index("sample") // 2


def column(row):
    i = lax.broadcasted_iota(jnp.int32, (OWN, OWN), 0)
    j = lax.broadcasted_iota(jnp.int32, (OWN, OWN), 1)
    return jnp.sum(jnp.where(i == j, jnp.broadcast_to(row, (OWN, OWN)), 0.0), axis=1, keepdims=True)


def dot(a, b, ca, cb):
    return lax.dot_general(a, b, (((ca,), (cb,)), ((), ())), preferred_element_type=F32)


def main_kernel(
    near_ref, far_ref, w2_ref, w1_ref, gain_ref, bias_ref,
    p_near, p_far, g0, g1, g2, g3,
    x_ref, dy_ref, act_ref, w2t_ref, taps_ref, rows_ref, whole_ref,
):
    me = lax.axis_index("tile")
    assemble(me, near_ref, far_ref, x_ref, 0)
    products = dot(w1_ref[...], x_ref[...].reshape(POS, CH), 1, 1)
    pre = jnp.zeros((OWN, POS), F32)
    for t, (dr, dc) in enumerate(TAPS):
        pre = pre + shifted(products[OWN * t : OWN * (t + 1)], dr, dc)
    count = 1.0 / (OWN * POS)
    mean = jnp.sum(pre, keepdims=True) * count
    centred = pre - mean
    rstd = lax.rsqrt(jnp.sum(centred * centred, keepdims=True) * count + 1e-05)
    xhat = centred * rstd
    gain = column(gain_ref[...])
    normed = xhat * gain + column(bias_ref[...])
    sig = jax.nn.sigmoid(normed)
    act = (normed * sig).astype(BF).astype(F32)
    for t, (dr, dc) in enumerate(TAPS):
        act_ref[OWN * t : OWN * (t + 1), :] = shifted(act, dr, dc).astype(BF)
    slope = sig * (1.0 + normed * (1.0 - sig))
    assemble(me, near_ref, far_ref, dy_ref, ROWS)
    xi = x_index()
    outs = (g0, g1, g2, g3)
    grad = dot(act_ref[...], dy_ref[...].reshape(POS, CH), 1, 0)
    split_blocks(xi, grad, whole_ref, outs, 9 * OWN + 16)
    for g in range(8):
        lanes = slice(128 * g, 128 * (g + 1))
        for t in range(8):
            rows, at = slice(OWN * (t // 4), OWN * (t // 4 + 1)), OWN * (t % 4)
            parts = [w2_ref[4 * g + j, rows, at : at + OWN].astype(F32) for j in range(4)]
            w2t_ref[OWN * t : OWN * (t + 1), lanes] = jnp.concatenate(parts, axis=1).astype(BF)
        tails = [w2_ref[4 * g + j, 2 * OWN :, :].astype(F32)[:8] for j in range(4)]
        parts = [jnp.concatenate([v[:, OWN * a : OWN * (a + 1)] for v in tails], axis=1) for a in range(4)]
        w2t_ref[8 * OWN :, lanes] = jnp.concatenate(parts, axis=0).astype(BF)
    products = dot(w2t_ref[...], dy_ref[...].reshape(POS, CH), 1, 1)
    act_grad = jnp.zeros((OWN, POS), F32)
    for t, (dr, dc) in enumerate(TAPS):
        act_grad = act_grad + shifted(products[OWN * t : OWN * (t + 1)], -dr, -dc)
    norm_grad = act_grad * slope
    gain_sum = jnp.sum(norm_grad * xhat, axis=1, keepdims=True)
    shift_sum = jnp.sum(norm_grad, axis=1, keepdims=True)
    scaled = norm_grad * gain
    count = 1.0 / (OWN * POS)
    first_mean = jnp.sum(scaled, keepdims=True) * count
    second_mean = jnp.sum(scaled * xhat, keepdims=True) * count
    pre_grad = rstd * (scaled - first_mean - xhat * second_mean)
    pre_grad = pre_grad.astype(BF).astype(F32)
    for t, (dr, dc) in enumerate(TAPS):
        taps_ref[OWN * t : OWN * (t + 1), :] = shifted(pre_grad, -dr, -dc)
    taps = taps_ref[...]
    grad = dot(taps.astype(BF), x_ref[...].reshape(POS, CH), 1, 0)
    split_blocks(xi, grad, whole_ref, outs, 0)
    high_g = gain_sum.astype(BF).astype(F32)
    high_s = shift_sum.astype(BF).astype(F32)
    lane = lax.broadcasted_iota(jnp.int32, (OWN, 128), 1)
    sums = jnp.where(lane == 0, high_g, 0.0) + jnp.where(lane == 1, gain_sum - high_g, 0.0)
    sums = sums + jnp.where(lane == 2, high_s, 0.0) + jnp.where(lane == 3, shift_sum - high_s, 0.0)
    extra = sums.T[:16, :]
    rows = slice(9 * OWN, 9 * OWN + 16)
    for out in outs:
        out[rows, :] = jnp.zeros((16, 256), out.dtype)
        out[rows, :OWN] = extra.astype(out.dtype)
    rows_ref[...] = taps.T
    half = len(SUM_ORDER) // 2
    for part, out in enumerate((p_near, p_far)):
        blocks = []
        for mask in SUM_ORDER[part * half : (part + 1) * half]:
            start = pl.multiple_of((me ^ mask) * ROWS, ROWS)
            blocks.append(rows_ref[pl.ds(start, ROWS), :])
        out[...] = dot(jnp.concatenate(blocks, axis=0).astype(BF), w1_ref[...], 1, 0)


def split_blocks(xi, grad, whole_ref, outs, at):
    whole_ref[...] = grad
    rows = slice(at, at + grad.shape[0])
    for m, out in enumerate(outs):
        lane = pl.multiple_of((xi ^ m) * 256, 256)
        out[rows, :] = whole_ref[:, pl.ds(lane, 256)].astype(out.dtype)


def turn_kernel(w_ref, out_ref):
    turned = w_ref[...].astype(F32).T
    out_ref[:, :OWN, :] = turned[:, :128].reshape(32, OWN, 128).astype(BF)
    out_ref[:, OWN : 2 * OWN, :] = turned[:, 128:256].reshape(32, OWN, 128).astype(BF)
    last = turned[:, 256:].reshape(32, 4, 8, OWN)
    last = jnp.concatenate([last[:, a] for a in range(4)], axis=2)
    out_ref[:, 2 * OWN :, :] = jnp.concatenate([last, jnp.zeros_like(last)], axis=1).astype(BF)


def finish_kernel(a0, a1, a2, a3, first_ref, second_ref, gain_ref, shift_ref):
    xi = x_index()
    sums = jnp.zeros((16, 256), F32)
    for m, part in enumerate((a0, a1, a2, a3)):
        lanes = pl.ds(pl.multiple_of((xi ^ m) * 256, 256), 256)
        first_ref[:, lanes] = part[: 9 * OWN, :].astype(F32)
        second_ref[:, lanes] = part[9 * OWN + 16 :, :].astype(F32)
        sums = jnp.where(xi == m, part[9 * OWN : 9 * OWN + 16, :].astype(F32), sums)
    gain_ref[...] = sums[0:1, :OWN] + sums[1:2, :OWN]
    shift_ref[...] = sums[2:3, :OWN] + sums[3:4, :OWN]


LIMIT = 14 * MB


def call(kernel, operands, outs, scratch=(), flops=0):
    vmem = pl.BlockSpec(memory_space=pltpu.VMEM)
    return pl.pallas_call(
        kernel,
        out_shape=[jax.ShapeDtypeStruct(s, d) for s, d in outs],
        in_specs=[vmem] * len(operands),
        out_specs=[vmem] * len(outs),
        scratch_shapes=[pltpu.VMEM(s, d) for s, d in scratch],
        compiler_params=pltpu.CompilerParams(vmem_limit_bytes=LIMIT),
        cost_estimate=pl.CostEstimate(flops=flops, bytes_accessed=4 * MB, transcendentals=0),
    )(*operands)


def resplit(total):
    gain = total[9 * OWN : 9 * OWN + 1] + total[9 * OWN + 1 : 9 * OWN + 2]
    shift = total[9 * OWN + 2 : 9 * OWN + 3] + total[9 * OWN + 3 : 9 * OWN + 4]
    high_g, high_s = gain.astype(BF).astype(F32), shift.astype(BF).astype(F32)
    row = lax.broadcasted_iota(jnp.int32, (16, 256), 0)
    extra = jnp.where(row == 0, high_g, 0.0) + jnp.where(row == 1, gain - high_g, 0.0)
    extra = extra + jnp.where(row == 2, high_s, 0.0) + jnp.where(row == 3, shift - high_s, 0.0)
    return extra.astype(BF)


def x_sum_kernel(own_ref, r1, r2, r3, out_ref):
    total = own_ref[...] + r1[...].astype(F32) + r2[...].astype(F32) + r3[...].astype(F32)
    out_ref[...] = total.astype(BF)
    out_ref[9 * OWN : 9 * OWN + 16, :] = resplit(total)


def z_sum_kernel(mine_ref, other_ref, out_ref):
    total = mine_ref[...].astype(F32) + other_ref[...].astype(F32)
    out_ref[...] = total.astype(BF)
    out_ref[9 * OWN : 9 * OWN + 16, :] = resplit(total)


def x_hops(parts):
    return [parts[0]] + [hop(parts[m], 2 * m, "sample", 8) for m in (1, 2, 3)]


def z_hop(mine):
    return hop(mine, 1, "sample", 8)


def spread(mine):
    return [mine] + [hop(mine, 2 * m, "sample", 8) for m in (1, 2, 3)]


def after(value, *others):
    return lax.optimization_barrier((value, *others))[0]


def per_device(inputs, first_weight, second_weight, norm_gain_vector, norm_bias, cotangent):
    w2 = second_weight.reshape(9 * OWN, CH)
    (turned,) = call(turn_kernel, [w2], [((32, 80, 128), BF)])
    block = jnp.concatenate([inputs.reshape(1, ROWS, CH), cotangent.reshape(1, ROWS, CH)], axis=1)
    held = jnp.concatenate([block] + [hop(block, m) for m in Z_MASKS])
    got = [hop(held, m) for m in Y_MASKS]
    w2_own = lax.all_to_all(after(turned, held), "tile", split_axis=0, concat_axis=0, tiled=True)
    near = jnp.concatenate([held] + got)
    far = hop(near, CORE)
    w1 = first_weight.reshape(9 * OWN, CH)
    gain, bias = norm_gain_vector.reshape(1, OWN), norm_bias.reshape(1, OWN)
    flops = 2 * 288 * POS * CH
    columns, taps, whole = (COLS, ROWS, CH), (9 * OWN, POS), (9 * OWN, CH)
    joint = (18 * OWN + 16, 256)
    conv_near, conv_far, *parts = call(
        main_kernel,
        [near, far, w2_own, w1, gain, bias],
        [((POS // 2, CH), F32)] * 2 + [(joint, F32)] + [(joint, BF)] * 3,
        [(columns, BF), (columns, BF), (taps, BF), (whole, BF), (taps, F32), ((POS, 9 * OWN), F32), (whole, F32)],
        5 * flops,
    )
    parts = x_hops(parts)
    conv_far = hop(conv_far, CORE)
    total = (conv_near + conv_far).reshape(4, POS // 8, CH)
    y_got = [hop(total[k].astype(BF), m) for k, m in zip((1, 2, 3), Y_MASKS)]
    (mine,) = call(x_sum_kernel, [after(parts[0], *y_got), *parts[1:]], [(joint, BF)])
    other = z_hop(mine)
    total = total[0] + y_got[0].astype(F32) + y_got[1].astype(F32) + y_got[2].astype(F32)
    total = after(total.reshape(4, ROWS, CH), other)
    z_got = [hop(total[k].astype(BF), m) for k, m in zip((1, 2, 3), Z_MASKS)]
    (summed,) = call(z_sum_kernel, [mine, other], [(joint, BF)])
    blocks = spread(summed)
    total = total[0] + z_got[0].astype(F32) + z_got[1].astype(F32) + z_got[2].astype(F32)
    conv_back = total.astype(BF).astype(F32)
    input_grad = (cotangent.reshape(ROWS, CH).astype(F32) + conv_back).astype(BF)
    grad, row = ((9 * OWN, CH), F32), ((1, OWN), F32)
    first_grad, second_grad, gain_grad, shift_grad = call(finish_kernel, blocks, [grad, grad, row, row])
    return (
        input_grad.reshape(1, ROWS, 1, CH),
        first_grad.reshape(9, OWN, CH),
        jnp.transpose(second_grad.reshape(9, OWN, CH), (0, 2, 1)),
        gain_grad.reshape(OWN),
        shift_grad.reshape(OWN),
    )


def solution(mesh):
    return jax.shard_map(
        per_device,
        mesh=mesh,
        in_specs=(
            P("sample", None, "tile", None),
            P(None, "tile", None),
            P(None, "tile", None),
            P("tile"),
            P("tile"),
            P("sample", None, "tile", None),
        ),
        out_specs=(
            P("sample", None, "tile", None),
            P(None, "tile", None),
            P(None, None, "tile"),
            P("tile"),
            P("tile"),
        ),
        check_vma=False,
    )
```

```python
import functools

import jax
import jax.numpy as jnp
from jax import lax
from jax.experimental import pallas as pl
from jax.experimental.pallas import tpu as pltpu
from jax.sharding import PartitionSpec as P

BF = jnp.bfloat16
F32 = jnp.float32
TAPS = [(dr, dc) for dr in (-1, 0, 1) for dc in (-1, 0, 1)]
ROWS, COLS, CH = 16, 32, 1024
POS = ROWS * COLS
OWN = 32
MB = 1 << 20

Z_MASKS, Y_MASKS, CORE = (8, 16, 24), (2, 4, 6), 1
ORDER = [c ^ y ^ z for c in (0, 1) for y in (0, 2, 4, 6) for z in (0, 8, 16, 24)]
SUM_ORDER = [c ^ y ^ z for c in (0, 1) for y in (0, 2, 4, 6) for z in (0, 8, 16, 24)]


def hop(value, mask, axis="tile", size=32):
    return lax.ppermute(value, axis, [(i, i ^ mask) for i in range(size)])


def shifted(value, dr, dc):
    step = ROWS * dc + dr
    moved = pltpu.roll(value, (-step) % POS, 1) if step else value
    if step == 0:
        return moved
    place = lax.broadcasted_iota(jnp.int32, value.shape, 1)
    row, col = place % ROWS + dr, place // ROWS + dc
    inside = (row >= 0) & (row < ROWS) & (col >= 0) & (col < COLS)
    return jnp.where(inside, moved, 0.0)


def assemble(me, near_ref, far_ref, out_ref, at):
    half = len(ORDER) // 2
    for k, mask in enumerate(ORDER):
        src = near_ref if k < half else far_ref
        out_ref[me ^ mask] = src[k % half, at : at + ROWS, :]


def x_index():
    return lax.axis_index("sample") // 2


def column(row):
    i = lax.broadcasted_iota(jnp.int32, (OWN, OWN), 0)
    j = lax.broadcasted_iota(jnp.int32, (OWN, OWN), 1)
    return jnp.sum(jnp.where(i == j, jnp.broadcast_to(row, (OWN, OWN)), 0.0), axis=1, keepdims=True)


def dot(a, b, ca, cb):
    return lax.dot_general(a, b, (((ca,), (cb,)), ((), ())), preferred_element_type=F32)


def main_kernel(
    near_ref, far_ref, w2_ref, w1_ref, gain_ref, bias_ref,
    p_near, p_far, g0, g1, g2, g3,
    x_ref, dy_ref, act_ref, w2t_ref, taps_ref, rows_ref, whole_ref,
):
    me = lax.axis_index("tile")
    assemble(me, near_ref, far_ref, x_ref, 0)
    products = dot(w1_ref[...], x_ref[...].reshape(POS, CH), 1, 1)
    pre = jnp.zeros((OWN, POS), F32)
    for t, (dr, dc) in enumerate(TAPS):
        pre = pre + shifted(products[OWN * t : OWN * (t + 1)], dr, dc)
    count = 1.0 / (OWN * POS)
    mean = jnp.sum(pre, keepdims=True) * count
    centred = pre - mean
    rstd = lax.rsqrt(jnp.sum(centred * centred, keepdims=True) * count + 1e-05)
    xhat = centred * rstd
    gain = column(gain_ref[...])
    normed = xhat * gain + column(bias_ref[...])
    sig = jax.nn.sigmoid(normed)
    act = (normed * sig).astype(BF).astype(F32)
    for t, (dr, dc) in enumerate(TAPS):
        act_ref[OWN * t : OWN * (t + 1), :] = shifted(act, dr, dc).astype(BF)
    slope = sig * (1.0 + normed * (1.0 - sig))
    assemble(me, near_ref, far_ref, dy_ref, ROWS)
    xi = x_index()
    outs = (g0, g1, g2, g3)
    grad = dot(act_ref[...], dy_ref[...].reshape(POS, CH), 1, 0)
    split_blocks(xi, grad, whole_ref, outs, 9 * OWN + 16)
    for g in range(8):
        lanes = slice(128 * g, 128 * (g + 1))
        came = [w2_ref[4 * g + j].astype(F32) for j in range(4)]
        for t in range(8):
            rows, at = slice(OWN * (t // 4), OWN * (t // 4 + 1)), OWN * (t % 4)
            parts = [v[rows, at : at + OWN] for v in came]
            w2t_ref[OWN * t : OWN * (t + 1), lanes] = jnp.concatenate(parts, axis=1).astype(BF)
        parts = [jnp.concatenate([v[2 * OWN :, OWN * a : OWN * (a + 1)] for v in came], axis=1) for a in range(4)]
        w2t_ref[8 * OWN :, lanes] = jnp.concatenate(parts, axis=0).astype(BF)
    products = dot(w2t_ref[...], dy_ref[...].reshape(POS, CH), 1, 1)
    act_grad = jnp.zeros((OWN, POS), F32)
    for t, (dr, dc) in enumerate(TAPS):
        act_grad = act_grad + shifted(products[OWN * t : OWN * (t + 1)], -dr, -dc)
    norm_grad = act_grad * slope
    gain_sum = jnp.sum(norm_grad * xhat, axis=1, keepdims=True)
    shift_sum = jnp.sum(norm_grad, axis=1, keepdims=True)
    scaled = norm_grad * gain
    count = 1.0 / (OWN * POS)
    first_mean = jnp.sum(scaled, keepdims=True) * count
    second_mean = jnp.sum(scaled * xhat, keepdims=True) * count
    pre_grad = rstd * (scaled - first_mean - xhat * second_mean)
    pre_grad = pre_grad.astype(BF).astype(F32)
    for t, (dr, dc) in enumerate(TAPS):
        taps_ref[OWN * t : OWN * (t + 1), :] = shifted(pre_grad, -dr, -dc)
    taps = taps_ref[...]
    grad = dot(taps.astype(BF), x_ref[...].reshape(POS, CH), 1, 0)
    split_blocks(xi, grad, whole_ref, outs, 0)
    high_g = gain_sum.astype(BF).astype(F32)
    high_s = shift_sum.astype(BF).astype(F32)
    lane = lax.broadcasted_iota(jnp.int32, (OWN, 128), 1)
    sums = jnp.where(lane == 0, high_g, 0.0) + jnp.where(lane == 1, gain_sum - high_g, 0.0)
    sums = sums + jnp.where(lane == 2, high_s, 0.0) + jnp.where(lane == 3, shift_sum - high_s, 0.0)
    extra = sums.T[:16, :]
    rows = slice(9 * OWN, 9 * OWN + 16)
    for out in outs:
        out[rows, :] = jnp.zeros((16, 256), out.dtype)
        out[rows, :OWN] = extra.astype(out.dtype)
    rows_ref[...] = taps.T
    half = len(SUM_ORDER) // 2
    for part, out in enumerate((p_near, p_far)):
        blocks = []
        for mask in SUM_ORDER[part * half : (part + 1) * half]:
            start = pl.multiple_of((me ^ mask) * ROWS, ROWS)
            blocks.append(rows_ref[pl.ds(start, ROWS), :])
        out[...] = dot(jnp.concatenate(blocks, axis=0).astype(BF), w1_ref[...], 1, 0)


def split_blocks(xi, grad, whole_ref, outs, at):
    whole_ref[...] = grad
    rows = slice(at, at + grad.shape[0])
    for m, out in enumerate(outs):
        lane = pl.multiple_of((xi ^ m) * 256, 256)
        out[rows, :] = whole_ref[:, pl.ds(lane, 256)].astype(out.dtype)


def turn_kernel(w_ref, out_ref):
    turned = w_ref[...].astype(F32).T
    last = turned[:, 256:].reshape(32, 4, 8, OWN)
    last = jnp.concatenate([last[:, a] for a in range(4)], axis=2)
    low, high = turned[:, :128].reshape(32, OWN, 128), turned[:, 128:256].reshape(32, OWN, 128)
    out_ref[...] = jnp.concatenate([low, high, last], axis=1).astype(BF)


def finish_kernel(a0, a1, a2, a3, first_ref, second_ref, gain_ref, shift_ref):
    xi = x_index()
    sums = jnp.zeros((16, 256), F32)
    for m, part in enumerate((a0, a1, a2, a3)):
        lanes = pl.ds(pl.multiple_of((xi ^ m) * 256, 256), 256)
        first_ref[:, lanes] = part[: 9 * OWN, :].astype(F32)
        second_ref[:, lanes] = part[9 * OWN + 16 :, :].astype(F32)
        sums = jnp.where(xi == m, part[9 * OWN : 9 * OWN + 16, :].astype(F32), sums)
    gain_ref[...] = sums[0:1, :OWN] + sums[1:2, :OWN]
    shift_ref[...] = sums[2:3, :OWN] + sums[3:4, :OWN]


LIMIT = 14 * MB


def call(kernel, operands, outs, scratch=(), flops=0):
    vmem = pl.BlockSpec(memory_space=pltpu.VMEM)
    return pl.pallas_call(
        kernel,
        out_shape=[jax.ShapeDtypeStruct(s, d) for s, d in outs],
        in_specs=[vmem] * len(operands),
        out_specs=[vmem] * len(outs),
        scratch_shapes=[pltpu.VMEM(s, d) for s, d in scratch],
        compiler_params=pltpu.CompilerParams(vmem_limit_bytes=LIMIT),
        cost_estimate=pl.CostEstimate(flops=flops, bytes_accessed=4 * MB, transcendentals=0),
    )(*operands)


def resplit(total):
    gain = total[9 * OWN : 9 * OWN + 1] + total[9 * OWN + 1 : 9 * OWN + 2]
    shift = total[9 * OWN + 2 : 9 * OWN + 3] + total[9 * OWN + 3 : 9 * OWN + 4]
    high_g, high_s = gain.astype(BF).astype(F32), shift.astype(BF).astype(F32)
    row = lax.broadcasted_iota(jnp.int32, (16, 256), 0)
    extra = jnp.where(row == 0, high_g, 0.0) + jnp.where(row == 1, gain - high_g, 0.0)
    extra = extra + jnp.where(row == 2, high_s, 0.0) + jnp.where(row == 3, shift - high_s, 0.0)
    return extra.astype(BF)


def x_sum_kernel(own_ref, r1, r2, r3, out_ref):
    total = own_ref[...] + r1[...].astype(F32) + r2[...].astype(F32) + r3[...].astype(F32)
    out_ref[...] = total.astype(BF)
    out_ref[9 * OWN : 9 * OWN + 16, :] = resplit(total)


def z_sum_kernel(mine_ref, other_ref, out_ref):
    total = mine_ref[...].astype(F32) + other_ref[...].astype(F32)
    out_ref[...] = total.astype(BF)
    out_ref[9 * OWN : 9 * OWN + 16, :] = resplit(total)


def x_hops(parts):
    return [parts[0]] + [hop(parts[m], 2 * m, "sample", 8) for m in (1, 2, 3)]


def z_hop(mine):
    return hop(mine, 1, "sample", 8)


def spread(mine):
    return [mine] + [hop(mine, 2 * m, "sample", 8) for m in (1, 2, 3)]


def after(value, *others):
    return lax.optimization_barrier((value, *others))[0]


def per_device(inputs, first_weight, second_weight, norm_gain_vector, norm_bias, cotangent):
    w2 = second_weight.reshape(9 * OWN, CH)
    (turned,) = call(turn_kernel, [w2], [((32, 72, 128), BF)])
    block = jnp.concatenate([inputs.reshape(1, ROWS, CH), cotangent.reshape(1, ROWS, CH)], axis=1)
    held = jnp.concatenate([block] + [hop(block, m) for m in Z_MASKS])
    got = [hop(held, m) for m in Y_MASKS]
    w2_own = lax.all_to_all(after(turned, held), "tile", split_axis=0, concat_axis=0, tiled=True)
    near = jnp.concatenate([held] + got)
    far = hop(near, CORE)
    w1 = first_weight.reshape(9 * OWN, CH)
    gain, bias = norm_gain_vector.reshape(1, OWN), norm_bias.reshape(1, OWN)
    flops = 2 * 288 * POS * CH
    columns, taps, whole = (COLS, ROWS, CH), (9 * OWN, POS), (9 * OWN, CH)
    joint = (18 * OWN + 16, 256)
    conv_near, conv_far, *parts = call(
        main_kernel,
        [near, far, w2_own, w1, gain, bias],
        [((POS // 2, CH), F32)] * 2 + [(joint, F32)] + [(joint, BF)] * 3,
        [(columns, BF), (columns, BF), (taps, BF), (whole, BF), (taps, F32), ((POS, 9 * OWN), F32), (whole, F32)],
        5 * flops,
    )
    parts = x_hops(parts)
    conv_far = hop(conv_far, CORE)
    total = (conv_near + conv_far).reshape(4, POS // 8, CH)
    y_got = [hop(total[k].astype(BF), m) for k, m in zip((1, 2, 3), Y_MASKS)]
    (mine,) = call(x_sum_kernel, [after(parts[0], *y_got), *parts[1:]], [(joint, BF)])
    other = z_hop(mine)
    total = total[0] + y_got[0].astype(F32) + y_got[1].astype(F32) + y_got[2].astype(F32)
    total = after(total.reshape(4, ROWS, CH), other)
    z_got = [hop(total[k].astype(BF), m) for k, m in zip((1, 2, 3), Z_MASKS)]
    (summed,) = call(z_sum_kernel, [mine, other], [(joint, BF)])
    blocks = spread(summed)
    total = total[0] + z_got[0].astype(F32) + z_got[1].astype(F32) + z_got[2].astype(F32)
    conv_back = total.astype(BF).astype(F32)
    input_grad = (cotangent.reshape(ROWS, CH).astype(F32) + conv_back).astype(BF)
    grad, row = ((9 * OWN, CH), F32), ((1, OWN), F32)
    first_grad, second_grad, gain_grad, shift_grad = call(finish_kernel, blocks, [grad, grad, row, row])
    return (
        input_grad.reshape(1, ROWS, 1, CH),
        first_grad.reshape(9, OWN, CH),
        jnp.transpose(second_grad.reshape(9, OWN, CH), (0, 2, 1)),
        gain_grad.reshape(OWN),
        shift_grad.reshape(OWN),
    )


def solution(mesh):
    return jax.shard_map(
        per_device,
        mesh=mesh,
        in_specs=(
            P("sample", None, "tile", None),
            P(None, "tile", None),
            P(None, "tile", None),
            P("tile"),
            P("tile"),
            P("sample", None, "tile", None),
        ),
        out_specs=(
            P("sample", None, "tile", None),
            P(None, "tile", None),
            P(None, None, "tile"),
            P("tile"),
            P("tile"),
        ),
        check_vma=False,
    )
```

```python
import functools

import jax
import jax.numpy as jnp
from jax import lax
from jax.experimental import pallas as pl
from jax.experimental.pallas import tpu as pltpu
from jax.sharding import PartitionSpec as P

BF = jnp.bfloat16
F32 = jnp.float32
TAPS = [(dr, dc) for dr in (-1, 0, 1) for dc in (-1, 0, 1)]
ROWS, COLS, CH = 16, 32, 1024
POS = ROWS * COLS
OWN = 32
MB = 1 << 20

Z_MASKS, Y_MASKS, CORE = (8, 16, 24), (2, 4, 6), 1
ORDER = [c ^ y ^ z for c in (0, 1) for y in (0, 2, 4, 6) for z in (0, 8, 16, 24)]
SUM_ORDER = [c ^ y ^ z for c in (0, 1) for y in (0, 2, 4, 6) for z in (0, 8, 16, 24)]


def hop(value, mask, axis="tile", size=32):
    return lax.ppermute(value, axis, [(i, i ^ mask) for i in range(size)])


def shifted(value, dr, dc):
    step = ROWS * dc + dr
    moved = pltpu.roll(value, (-step) % POS, 1) if step else value
    if step == 0:
        return moved
    place = lax.broadcasted_iota(jnp.int32, value.shape, 1)
    row, col = place % ROWS + dr, place // ROWS + dc
    inside = (row >= 0) & (row < ROWS) & (col >= 0) & (col < COLS)
    return jnp.where(inside, moved, 0.0)


def assemble(me, near_ref, far_ref, out_ref, at):
    half = len(ORDER) // 2
    for k, mask in enumerate(ORDER):
        src = near_ref if k < half else far_ref
        out_ref[me ^ mask] = src[k % half, at : at + ROWS, :]


def x_index():
    return lax.axis_index("sample") // 2


def column(row):
    i = lax.broadcasted_iota(jnp.int32, (OWN, OWN), 0)
    j = lax.broadcasted_iota(jnp.int32, (OWN, OWN), 1)
    return jnp.sum(jnp.where(i == j, jnp.broadcast_to(row, (OWN, OWN)), 0.0), axis=1, keepdims=True)


def dot(a, b, ca, cb):
    return lax.dot_general(a, b, (((ca,), (cb,)), ((), ())), preferred_element_type=F32)


def forward_kernel(near_ref, far_ref, w1_ref, state_ref, x_ref):
    assemble(lax.axis_index("tile"), near_ref, far_ref, x_ref, 0)
    products = dot(w1_ref[...], x_ref[...].reshape(POS, CH), 1, 1)
    pre = jnp.zeros((OWN, POS), F32)
    for t, (dr, dc) in enumerate(TAPS):
        pre = pre + shifted(products[OWN * t : OWN * (t + 1)], dr, dc)
    count = 1.0 / (OWN * POS)
    mean = jnp.sum(pre, keepdims=True) * count
    centred = pre - mean
    rstd = lax.rsqrt(jnp.sum(centred * centred, keepdims=True) * count + 1e-05)
    state_ref[:OWN, :] = centred * rstd
    state_ref[OWN:, :] = jnp.broadcast_to(rstd, (8, POS))


def main_kernel(
    near_ref, far_ref, w2_ref, w1_ref, gain_ref, bias_ref, state_ref,
    p_near, p_far, g0, g1, g2, g3,
    x_ref, dy_ref, act_ref, w2t_ref, taps_ref, rows_ref, whole_ref,
):
    me = lax.axis_index("tile")
    assemble(me, near_ref, far_ref, x_ref, 0)
    xhat = state_ref[:OWN, :]
    rstd = state_ref[OWN : OWN + 1, 0:1]
    gain = column(gain_ref[...])
    normed = xhat * gain + column(bias_ref[...])
    sig = jax.nn.sigmoid(normed)
    act = (normed * sig).astype(BF).astype(F32)
    for t, (dr, dc) in enumerate(TAPS):
        act_ref[OWN * t : OWN * (t + 1), :] = shifted(act, dr, dc).astype(BF)
    slope = sig * (1.0 + normed * (1.0 - sig))
    assemble(me, near_ref, far_ref, dy_ref, ROWS)
    xi = x_index()
    outs = (g0, g1, g2, g3)
    grad = dot(act_ref[...], dy_ref[...].reshape(POS, CH), 1, 0)
    split_blocks(xi, grad, whole_ref, outs, 9 * OWN + 16)
    for g in range(8):
        lanes = slice(128 * g, 128 * (g + 1))
        came = [w2_ref[4 * g + j].astype(F32) for j in range(4)]
        for t in range(8):
            rows, at = slice(OWN * (t // 4), OWN * (t // 4 + 1)), OWN * (t % 4)
            parts = [v[rows, at : at + OWN] for v in came]
            w2t_ref[OWN * t : OWN * (t + 1), lanes] = jnp.concatenate(parts, axis=1).astype(BF)
        parts = [jnp.concatenate([v[2 * OWN :, OWN * a : OWN * (a + 1)] for v in came], axis=1) for a in range(4)]
        w2t_ref[8 * OWN :, lanes] = jnp.concatenate(parts, axis=0).astype(BF)
    products = dot(w2t_ref[...], dy_ref[...].reshape(POS, CH), 1, 1)
    act_grad = jnp.zeros((OWN, POS), F32)
    for t, (dr, dc) in enumerate(TAPS):
        act_grad = act_grad + shifted(products[OWN * t : OWN * (t + 1)], -dr, -dc)
    norm_grad = act_grad * slope
    gain_sum = jnp.sum(norm_grad * xhat, axis=1, keepdims=True)
    shift_sum = jnp.sum(norm_grad, axis=1, keepdims=True)
    scaled = norm_grad * gain
    count = 1.0 / (OWN * POS)
    first_mean = jnp.sum(scaled, keepdims=True) * count
    second_mean = jnp.sum(scaled * xhat, keepdims=True) * count
    pre_grad = rstd * (scaled - first_mean - xhat * second_mean)
    pre_grad = pre_grad.astype(BF).astype(F32)
    for t, (dr, dc) in enumerate(TAPS):
        taps_ref[OWN * t : OWN * (t + 1), :] = shifted(pre_grad, -dr, -dc)
    taps = taps_ref[...]
    grad = dot(taps.astype(BF), x_ref[...].reshape(POS, CH), 1, 0)
    split_blocks(xi, grad, whole_ref, outs, 0)
    high_g = gain_sum.astype(BF).astype(F32)
    high_s = shift_sum.astype(BF).astype(F32)
    lane = lax.broadcasted_iota(jnp.int32, (OWN, 128), 1)
    sums = jnp.where(lane == 0, high_g, 0.0) + jnp.where(lane == 1, gain_sum - high_g, 0.0)
    sums = sums + jnp.where(lane == 2, high_s, 0.0) + jnp.where(lane == 3, shift_sum - high_s, 0.0)
    extra = sums.T[:16, :]
    rows = slice(9 * OWN, 9 * OWN + 16)
    for out in outs:
        out[rows, :] = jnp.zeros((16, 256), out.dtype)
        out[rows, :OWN] = extra.astype(out.dtype)
    rows_ref[...] = taps.T
    half = len(SUM_ORDER) // 2
    for part, out in enumerate((p_near, p_far)):
        blocks = []
        for mask in SUM_ORDER[part * half : (part + 1) * half]:
            start = pl.multiple_of((me ^ mask) * ROWS, ROWS)
            blocks.append(rows_ref[pl.ds(start, ROWS), :])
        out[...] = dot(jnp.concatenate(blocks, axis=0).astype(BF), w1_ref[...], 1, 0)


def split_blocks(xi, grad, whole_ref, outs, at):
    whole_ref[...] = grad
    rows = slice(at, at + grad.shape[0])
    for m, out in enumerate(outs):
        lane = pl.multiple_of((xi ^ m) * 256, 256)
        out[rows, :] = whole_ref[:, pl.ds(lane, 256)].astype(out.dtype)


def turn_kernel(w_ref, out_ref):
    turned = w_ref[...].astype(F32).T
    last = turned[:, 256:].reshape(32, 4, 8, OWN)
    last = jnp.concatenate([last[:, a] for a in range(4)], axis=2)
    low, high = turned[:, :128].reshape(32, OWN, 128), turned[:, 128:256].reshape(32, OWN, 128)
    out_ref[...] = jnp.concatenate([low, high, last], axis=1).astype(BF)


def finish_kernel(a0, a1, a2, a3, first_ref, second_ref, gain_ref, shift_ref):
    xi = x_index()
    sums = jnp.zeros((16, 256), F32)
    for m, part in enumerate((a0, a1, a2, a3)):
        lanes = pl.ds(pl.multiple_of((xi ^ m) * 256, 256), 256)
        first_ref[:, lanes] = part[: 9 * OWN, :].astype(F32)
        second_ref[:, lanes] = part[9 * OWN + 16 :, :].astype(F32)
        sums = jnp.where(xi == m, part[9 * OWN : 9 * OWN + 16, :].astype(F32), sums)
    gain_ref[...] = sums[0:1, :OWN] + sums[1:2, :OWN]
    shift_ref[...] = sums[2:3, :OWN] + sums[3:4, :OWN]


LIMIT = 14 * MB


def call(kernel, operands, outs, scratch=(), flops=0):
    vmem = pl.BlockSpec(memory_space=pltpu.VMEM)
    return pl.pallas_call(
        kernel,
        out_shape=[jax.ShapeDtypeStruct(s, d) for s, d in outs],
        in_specs=[vmem] * len(operands),
        out_specs=[vmem] * len(outs),
        scratch_shapes=[pltpu.VMEM(s, d) for s, d in scratch],
        compiler_params=pltpu.CompilerParams(vmem_limit_bytes=LIMIT),
        cost_estimate=pl.CostEstimate(flops=flops, bytes_accessed=4 * MB, transcendentals=0),
    )(*operands)


def resplit(total):
    gain = total[9 * OWN : 9 * OWN + 1] + total[9 * OWN + 1 : 9 * OWN + 2]
    shift = total[9 * OWN + 2 : 9 * OWN + 3] + total[9 * OWN + 3 : 9 * OWN + 4]
    high_g, high_s = gain.astype(BF).astype(F32), shift.astype(BF).astype(F32)
    row = lax.broadcasted_iota(jnp.int32, (16, 256), 0)
    extra = jnp.where(row == 0, high_g, 0.0) + jnp.where(row == 1, gain - high_g, 0.0)
    extra = extra + jnp.where(row == 2, high_s, 0.0) + jnp.where(row == 3, shift - high_s, 0.0)
    return extra.astype(BF)


def x_sum_kernel(own_ref, r1, r2, r3, out_ref):
    total = own_ref[...] + r1[...].astype(F32) + r2[...].astype(F32) + r3[...].astype(F32)
    out_ref[...] = total.astype(BF)
    out_ref[9 * OWN : 9 * OWN + 16, :] = resplit(total)


def z_sum_kernel(mine_ref, other_ref, out_ref):
    total = mine_ref[...].astype(F32) + other_ref[...].astype(F32)
    out_ref[...] = total.astype(BF)
    out_ref[9 * OWN : 9 * OWN + 16, :] = resplit(total)


def x_hops(parts):
    return [parts[0]] + [hop(parts[m], 2 * m, "sample", 8) for m in (1, 2, 3)]


def z_hop(mine):
    return hop(mine, 1, "sample", 8)


def spread(mine):
    return [mine] + [hop(mine, 2 * m, "sample", 8) for m in (1, 2, 3)]


def after(value, *others):
    return lax.optimization_barrier((value, *others))[0]


def per_device(inputs, first_weight, second_weight, norm_gain_vector, norm_bias, cotangent):
    w2 = second_weight.reshape(9 * OWN, CH)
    (turned,) = call(turn_kernel, [w2], [((32, 72, 128), BF)])
    block = jnp.concatenate([inputs.reshape(1, ROWS, CH), cotangent.reshape(1, ROWS, CH)], axis=1)
    held = jnp.concatenate([block] + [hop(block, m) for m in Z_MASKS])
    got = [hop(held, m) for m in Y_MASKS]
    w2_own = lax.all_to_all(after(turned, held), "tile", split_axis=0, concat_axis=0, tiled=True)
    near = jnp.concatenate([held] + got)
    far = hop(near, CORE)
    w1 = first_weight.reshape(9 * OWN, CH)
    gain, bias = norm_gain_vector.reshape(1, OWN), norm_bias.reshape(1, OWN)
    flops = 2 * 288 * POS * CH
    columns, taps, whole = (COLS, ROWS, CH), (9 * OWN, POS), (9 * OWN, CH)
    joint = (18 * OWN + 16, 256)
    (state,) = call(forward_kernel, [near, far, w1], [((OWN + 8, POS), F32)], [(columns, BF)], flops)
    conv_near, conv_far, *parts = call(
        main_kernel,
        [near, far, w2_own, w1, gain, bias, state],
        [((POS // 2, CH), F32)] * 2 + [(joint, F32)] + [(joint, BF)] * 3,
        [(columns, BF), (columns, BF), (taps, BF), (whole, BF), (taps, F32), ((POS, 9 * OWN), F32), (whole, F32)],
        4 * flops,
    )
    parts = x_hops(parts)
    conv_far = hop(conv_far, CORE)
    total = (conv_near + conv_far).reshape(4, POS // 8, CH)
    y_got = [hop(total[k].astype(BF), m) for k, m in zip((1, 2, 3), Y_MASKS)]
    (mine,) = call(x_sum_kernel, [after(parts[0], *y_got), *parts[1:]], [(joint, BF)])
    other = z_hop(mine)
    total = total[0] + y_got[0].astype(F32) + y_got[1].astype(F32) + y_got[2].astype(F32)
    total = after(total.reshape(4, ROWS, CH), other)
    z_got = [hop(total[k].astype(BF), m) for k, m in zip((1, 2, 3), Z_MASKS)]
    (summed,) = call(z_sum_kernel, [mine, other], [(joint, BF)])
    blocks = spread(summed)
    total = total[0] + z_got[0].astype(F32) + z_got[1].astype(F32) + z_got[2].astype(F32)
    conv_back = total.astype(BF).astype(F32)
    input_grad = (cotangent.reshape(ROWS, CH).astype(F32) + conv_back).astype(BF)
    grad, row = ((9 * OWN, CH), F32), ((1, OWN), F32)
    first_grad, second_grad, gain_grad, shift_grad = call(finish_kernel, blocks, [grad, grad, row, row])
    return (
        input_grad.reshape(1, ROWS, 1, CH),
        first_grad.reshape(9, OWN, CH),
        jnp.transpose(second_grad.reshape(9, OWN, CH), (0, 2, 1)),
        gain_grad.reshape(OWN),
        shift_grad.reshape(OWN),
    )


def solution(mesh):
    return jax.shard_map(
        per_device,
        mesh=mesh,
        in_specs=(
            P("sample", None, "tile", None),
            P(None, "tile", None),
            P(None, "tile", None),
            P("tile"),
            P("tile"),
            P("sample", None, "tile", None),
        ),
        out_specs=(
            P("sample", None, "tile", None),
            P(None, "tile", None),
            P(None, None, "tile"),
            P("tile"),
            P("tile"),
        ),
        check_vma=False,
    )
```

```python
import functools

import jax
import jax.numpy as jnp
from jax import lax
from jax.experimental import pallas as pl
from jax.experimental.pallas import tpu as pltpu
from jax.sharding import PartitionSpec as P

BF = jnp.bfloat16
F32 = jnp.float32
TAPS = [(dr, dc) for dr in (-1, 0, 1) for dc in (-1, 0, 1)]
ROWS, COLS, CH = 16, 32, 1024
POS = ROWS * COLS
OWN = 32
MB = 1 << 20

Z_MASKS, Y_MASKS, CORE = (8, 16, 24), (2, 4, 6), 1
ORDER = [c ^ y ^ z for c in (0, 1) for y in (0, 2, 4, 6) for z in (0, 8, 16, 24)]
SUM_ORDER = [c ^ y ^ z for c in (0, 1) for y in (0, 2, 4, 6) for z in (0, 8, 16, 24)]


def hop(value, mask, axis="tile", size=32):
    return lax.ppermute(value, axis, [(i, i ^ mask) for i in range(size)])


def shifted(value, dr, dc):
    step = ROWS * dc + dr
    moved = pltpu.roll(value, (-step) % POS, 1) if step else value
    if step == 0:
        return moved
    place = lax.broadcasted_iota(jnp.int32, value.shape, 1)
    row, col = place % ROWS + dr, place // ROWS + dc
    inside = (row >= 0) & (row < ROWS) & (col >= 0) & (col < COLS)
    return jnp.where(inside, moved, 0.0)


def assemble(me, near_ref, far_ref, out_ref, at):
    half = len(ORDER) // 2
    for k, mask in enumerate(ORDER):
        src = near_ref if k < half else far_ref
        out_ref[me ^ mask] = src[k % half, at : at + ROWS, :]


def x_index():
    return lax.axis_index("sample") // 2


def column(row):
    i = lax.broadcasted_iota(jnp.int32, (OWN, OWN), 0)
    j = lax.broadcasted_iota(jnp.int32, (OWN, OWN), 1)
    return jnp.sum(jnp.where(i == j, jnp.broadcast_to(row, (OWN, OWN)), 0.0), axis=1, keepdims=True)


def dot(a, b, ca, cb):
    return lax.dot_general(a, b, (((ca,), (cb,)), ((), ())), preferred_element_type=F32)


def forward_kernel(near_ref, far_ref, w1_ref, state_ref, x_ref):
    assemble(lax.axis_index("tile"), near_ref, far_ref, x_ref, 0)
    products = dot(w1_ref[...], x_ref[...].reshape(POS, CH), 1, 1)
    pre = jnp.zeros((OWN, POS), F32)
    for t, (dr, dc) in enumerate(TAPS):
        pre = pre + shifted(products[OWN * t : OWN * (t + 1)], dr, dc)
    count = 1.0 / (OWN * POS)
    mean = jnp.sum(pre, keepdims=True) * count
    centred = pre - mean
    rstd = lax.rsqrt(jnp.sum(centred * centred, keepdims=True) * count + 1e-05)
    state_ref[:OWN, :] = centred * rstd
    state_ref[OWN:, :] = jnp.broadcast_to(rstd, (8, POS))


def main_kernel(
    near_ref, far_ref, w2_ref, gain_ref, bias_ref, state_ref,
    taps_ref, g0, g1, g2, g3,
    x_ref, dy_ref, act_ref, w2t_ref, whole_ref,
):
    me = lax.axis_index("tile")
    assemble(me, near_ref, far_ref, x_ref, 0)
    xhat = state_ref[:OWN, :]
    rstd = state_ref[OWN : OWN + 1, 0:1]
    gain = column(gain_ref[...])
    normed = xhat * gain + column(bias_ref[...])
    sig = jax.nn.sigmoid(normed)
    act = (normed * sig).astype(BF).astype(F32)
    for t, (dr, dc) in enumerate(TAPS):
        act_ref[OWN * t : OWN * (t + 1), :] = shifted(act, dr, dc).astype(BF)
    slope = sig * (1.0 + normed * (1.0 - sig))
    assemble(me, near_ref, far_ref, dy_ref, ROWS)
    xi = x_index()
    outs = (g0, g1, g2, g3)
    grad = dot(act_ref[...], dy_ref[...].reshape(POS, CH), 1, 0)
    split_blocks(xi, grad, whole_ref, outs, 9 * OWN + 16)
    for g in range(8):
        lanes = slice(128 * g, 128 * (g + 1))
        came = [w2_ref[4 * g + j].astype(F32) for j in range(4)]
        for t in range(8):
            rows, at = slice(OWN * (t // 4), OWN * (t // 4 + 1)), OWN * (t % 4)
            parts = [v[rows, at : at + OWN] for v in came]
            w2t_ref[OWN * t : OWN * (t + 1), lanes] = jnp.concatenate(parts, axis=1).astype(BF)
        parts = [jnp.concatenate([v[2 * OWN :, OWN * a : OWN * (a + 1)] for v in came], axis=1) for a in range(4)]
        w2t_ref[8 * OWN :, lanes] = jnp.concatenate(parts, axis=0).astype(BF)
    products = dot(w2t_ref[...], dy_ref[...].reshape(POS, CH), 1, 1)
    act_grad = jnp.zeros((OWN, POS), F32)
    for t, (dr, dc) in enumerate(TAPS):
        act_grad = act_grad + shifted(products[OWN * t : OWN * (t + 1)], -dr, -dc)
    norm_grad = act_grad * slope
    gain_sum = jnp.sum(norm_grad * xhat, axis=1, keepdims=True)
    shift_sum = jnp.sum(norm_grad, axis=1, keepdims=True)
    scaled = norm_grad * gain
    count = 1.0 / (OWN * POS)
    first_mean = jnp.sum(scaled, keepdims=True) * count
    second_mean = jnp.sum(scaled * xhat, keepdims=True) * count
    pre_grad = rstd * (scaled - first_mean - xhat * second_mean)
    pre_grad = pre_grad.astype(BF).astype(F32)
    for t, (dr, dc) in enumerate(TAPS):
        taps_ref[OWN * t : OWN * (t + 1), :] = shifted(pre_grad, -dr, -dc)
    taps = taps_ref[...]
    grad = dot(taps.astype(BF), x_ref[...].reshape(POS, CH), 1, 0)
    split_blocks(xi, grad, whole_ref, outs, 0)
    high_g = gain_sum.astype(BF).astype(F32)
    high_s = shift_sum.astype(BF).astype(F32)
    lane = lax.broadcasted_iota(jnp.int32, (OWN, 128), 1)
    sums = jnp.where(lane == 0, high_g, 0.0) + jnp.where(lane == 1, gain_sum - high_g, 0.0)
    sums = sums + jnp.where(lane == 2, high_s, 0.0) + jnp.where(lane == 3, shift_sum - high_s, 0.0)
    extra = sums.T[:16, :]
    rows = slice(9 * OWN, 9 * OWN + 16)
    for out in outs:
        out[rows, :] = jnp.zeros((16, 256), out.dtype)
        out[rows, :OWN] = extra.astype(out.dtype)


def conv_kernel(taps_ref, w1_ref, p_near, p_far, rows_ref):
    me = lax.axis_index("tile")
    rows_ref[...] = taps_ref[...].T
    half = len(SUM_ORDER) // 2
    for part, out in enumerate((p_near, p_far)):
        blocks = []
        for mask in SUM_ORDER[part * half : (part + 1) * half]:
            start = pl.multiple_of((me ^ mask) * ROWS, ROWS)
            blocks.append(rows_ref[pl.ds(start, ROWS), :])
        out[...] = dot(jnp.concatenate(blocks, axis=0).astype(BF), w1_ref[...], 1, 0)


def split_blocks(xi, grad, whole_ref, outs, at):
    whole_ref[...] = grad
    rows = slice(at, at + grad.shape[0])
    for m, out in enumerate(outs):
        lane = pl.multiple_of((xi ^ m) * 256, 256)
        out[rows, :] = whole_ref[:, pl.ds(lane, 256)].astype(out.dtype)


def turn_kernel(w_ref, out_ref):
    turned = w_ref[...].astype(F32).T
    last = turned[:, 256:].reshape(32, 4, 8, OWN)
    last = jnp.concatenate([last[:, a] for a in range(4)], axis=2)
    low, high = turned[:, :128].reshape(32, OWN, 128), turned[:, 128:256].reshape(32, OWN, 128)
    out_ref[...] = jnp.concatenate([low, high, last], axis=1).astype(BF)


def finish_kernel(a0, a1, a2, a3, first_ref, second_ref, gain_ref, shift_ref):
    xi = x_index()
    sums = jnp.zeros((16, 256), F32)
    for m, part in enumerate((a0, a1, a2, a3)):
        lanes = pl.ds(pl.multiple_of((xi ^ m) * 256, 256), 256)
        first_ref[:, lanes] = part[: 9 * OWN, :].astype(F32)
        second_ref[:, lanes] = part[9 * OWN + 16 :, :].astype(F32)
        sums = jnp.where(xi == m, part[9 * OWN : 9 * OWN + 16, :].astype(F32), sums)
    gain_ref[...] = sums[0:1, :OWN] + sums[1:2, :OWN]
    shift_ref[...] = sums[2:3, :OWN] + sums[3:4, :OWN]


LIMIT = 14 * MB


def call(kernel, operands, outs, scratch=(), flops=0):
    vmem = pl.BlockSpec(memory_space=pltpu.VMEM)
    return pl.pallas_call(
        kernel,
        out_shape=[jax.ShapeDtypeStruct(s, d) for s, d in outs],
        in_specs=[vmem] * len(operands),
        out_specs=[vmem] * len(outs),
        scratch_shapes=[pltpu.VMEM(s, d) for s, d in scratch],
        compiler_params=pltpu.CompilerParams(vmem_limit_bytes=LIMIT),
        cost_estimate=pl.CostEstimate(flops=flops, bytes_accessed=4 * MB, transcendentals=0),
    )(*operands)


def resplit(total):
    gain = total[9 * OWN : 9 * OWN + 1] + total[9 * OWN + 1 : 9 * OWN + 2]
    shift = total[9 * OWN + 2 : 9 * OWN + 3] + total[9 * OWN + 3 : 9 * OWN + 4]
    high_g, high_s = gain.astype(BF).astype(F32), shift.astype(BF).astype(F32)
    row = lax.broadcasted_iota(jnp.int32, (16, 256), 0)
    extra = jnp.where(row == 0, high_g, 0.0) + jnp.where(row == 1, gain - high_g, 0.0)
    extra = extra + jnp.where(row == 2, high_s, 0.0) + jnp.where(row == 3, shift - high_s, 0.0)
    return extra.astype(BF)


def x_sum_kernel(own_ref, r1, r2, r3, out_ref):
    total = own_ref[...] + r1[...].astype(F32) + r2[...].astype(F32) + r3[...].astype(F32)
    out_ref[...] = total.astype(BF)
    out_ref[9 * OWN : 9 * OWN + 16, :] = resplit(total)


def z_sum_kernel(mine_ref, other_ref, out_ref):
    total = mine_ref[...].astype(F32) + other_ref[...].astype(F32)
    out_ref[...] = total.astype(BF)
    out_ref[9 * OWN : 9 * OWN + 16, :] = resplit(total)


def x_hops(parts):
    return [parts[0]] + [hop(parts[m], 2 * m, "sample", 8) for m in (1, 2, 3)]


def z_hop(mine):
    return hop(mine, 1, "sample", 8)


def spread(mine):
    return [mine] + [hop(mine, 2 * m, "sample", 8) for m in (1, 2, 3)]


def after(value, *others):
    return lax.optimization_barrier((value, *others))[0]


def per_device(inputs, first_weight, second_weight, norm_gain_vector, norm_bias, cotangent):
    w2 = second_weight.reshape(9 * OWN, CH)
    (turned,) = call(turn_kernel, [w2], [((32, 72, 128), BF)])
    block = jnp.concatenate([inputs.reshape(1, ROWS, CH), cotangent.reshape(1, ROWS, CH)], axis=1)
    held = jnp.concatenate([block] + [hop(block, m) for m in Z_MASKS])
    got = [hop(held, m) for m in Y_MASKS]
    w2_own = lax.all_to_all(after(turned, held), "tile", split_axis=0, concat_axis=0, tiled=True)
    near = jnp.concatenate([held] + got)
    far = hop(near, CORE)
    w1 = first_weight.reshape(9 * OWN, CH)
    gain, bias = norm_gain_vector.reshape(1, OWN), norm_bias.reshape(1, OWN)
    flops = 2 * 288 * POS * CH
    columns, taps, whole = (COLS, ROWS, CH), (9 * OWN, POS), (9 * OWN, CH)
    joint = (18 * OWN + 16, 256)
    (state,) = call(forward_kernel, [near, far, w1], [((OWN + 8, POS), F32)], [(columns, BF)], flops)
    pre_taps, *parts = call(
        main_kernel,
        [near, far, w2_own, gain, bias, state],
        [(taps, F32), (joint, F32)] + [(joint, BF)] * 3,
        [(columns, BF), (columns, BF), (taps, BF), (whole, BF), (whole, F32)],
        3 * flops,
    )
    parts = x_hops(parts)
    conv_near, conv_far = call(conv_kernel, [after(pre_taps, *parts[1:]), w1], [((POS // 2, CH), F32)] * 2, [((POS, 9 * OWN), F32)], flops)
    conv_far = hop(conv_far, CORE)
    total = (conv_near + conv_far).reshape(4, POS // 8, CH)
    y_got = [hop(total[k].astype(BF), m) for k, m in zip((1, 2, 3), Y_MASKS)]
    (mine,) = call(x_sum_kernel, parts, [(joint, BF)])
    other = z_hop(mine)
    total = total[0] + y_got[0].astype(F32) + y_got[1].astype(F32) + y_got[2].astype(F32)
    total = after(total.reshape(4, ROWS, CH), other)
    z_got = [hop(total[k].astype(BF), m) for k, m in zip((1, 2, 3), Z_MASKS)]
    (summed,) = call(z_sum_kernel, [after(mine, *y_got), other], [(joint, BF)])
    blocks = spread(summed)
    total = total[0] + z_got[0].astype(F32) + z_got[1].astype(F32) + z_got[2].astype(F32)
    conv_back = total.astype(BF).astype(F32)
    input_grad = (cotangent.reshape(ROWS, CH).astype(F32) + conv_back).astype(BF)
    grad, row = ((9 * OWN, CH), F32), ((1, OWN), F32)
    first_grad, second_grad, gain_grad, shift_grad = call(finish_kernel, blocks, [grad, grad, row, row])
    return (
        input_grad.reshape(1, ROWS, 1, CH),
        first_grad.reshape(9, OWN, CH),
        jnp.transpose(second_grad.reshape(9, OWN, CH), (0, 2, 1)),
        gain_grad.reshape(OWN),
        shift_grad.reshape(OWN),
    )


def solution(mesh):
    return jax.shard_map(
        per_device,
        mesh=mesh,
        in_specs=(
            P("sample", None, "tile", None),
            P(None, "tile", None),
            P(None, "tile", None),
            P("tile"),
            P("tile"),
            P("sample", None, "tile", None),
        ),
        out_specs=(
            P("sample", None, "tile", None),
            P(None, "tile", None),
            P(None, None, "tile"),
            P("tile"),
            P("tile"),
        ),
        check_vma=False,
    )
```

```python
import functools

import jax
import jax.numpy as jnp
from jax import lax
from jax.experimental import pallas as pl
from jax.experimental.pallas import tpu as pltpu
from jax.sharding import PartitionSpec as P

BF = jnp.bfloat16
F32 = jnp.float32
TAPS = [(dr, dc) for dr in (-1, 0, 1) for dc in (-1, 0, 1)]
ROWS, COLS, CH = 16, 32, 1024
POS = ROWS * COLS
OWN = 32
MB = 1 << 20

Z_MASKS, Y_MASKS, CORE = (8, 16, 24), (2, 4, 6), 1
ORDER = [c ^ y ^ z for c in (0, 1) for y in (0, 2, 4, 6) for z in (0, 8, 16, 24)]
SUM_ORDER = [c ^ y ^ z for c in (0, 1) for y in (0, 2, 4, 6) for z in (0, 8, 16, 24)]


def hop(value, mask, axis="tile", size=32):
    return lax.ppermute(value, axis, [(i, i ^ mask) for i in range(size)])


def shifted(value, dr, dc):
    step = ROWS * dc + dr
    moved = pltpu.roll(value, (-step) % POS, 1) if step else value
    if step == 0:
        return moved
    place = lax.broadcasted_iota(jnp.int32, value.shape, 1)
    row, col = place % ROWS + dr, place // ROWS + dc
    inside = (row >= 0) & (row < ROWS) & (col >= 0) & (col < COLS)
    return jnp.where(inside, moved, 0.0)


def assemble(me, near_ref, far_ref, out_ref, at):
    half = len(ORDER) // 2
    for k, mask in enumerate(ORDER):
        src = near_ref if k < half else far_ref
        out_ref[me ^ mask] = src[k % half, at : at + ROWS, :]


def x_index():
    return lax.axis_index("sample") // 2


def column(row):
    i = lax.broadcasted_iota(jnp.int32, (OWN, OWN), 0)
    j = lax.broadcasted_iota(jnp.int32, (OWN, OWN), 1)
    return jnp.sum(jnp.where(i == j, jnp.broadcast_to(row, (OWN, OWN)), 0.0), axis=1, keepdims=True)


def dot(a, b, ca, cb):
    return lax.dot_general(a, b, (((ca,), (cb,)), ((), ())), preferred_element_type=F32)


def forward_kernel(near_ref, far_ref, w1_ref, state_ref, x_ref):
    assemble(lax.axis_index("tile"), near_ref, far_ref, x_ref, 0)
    products = dot(w1_ref[...], x_ref[...].reshape(POS, CH), 1, 1)
    pre = jnp.zeros((OWN, POS), F32)
    for t, (dr, dc) in enumerate(TAPS):
        pre = pre + shifted(products[OWN * t : OWN * (t + 1)], dr, dc)
    count = 1.0 / (OWN * POS)
    mean = jnp.sum(pre, keepdims=True) * count
    centred = pre - mean
    rstd = lax.rsqrt(jnp.sum(centred * centred, keepdims=True) * count + 1e-05)
    state_ref[:OWN, :] = centred * rstd
    state_ref[OWN:, :] = jnp.broadcast_to(rstd, (8, POS))


def main_kernel(
    near_ref, far_ref, w2_ref, w1_ref, gain_ref, bias_ref, state_ref,
    p_near, p_far, g0, g1, g2, g3,
    x_ref, dy_ref, act_ref, w2t_ref, taps_ref, rows_ref, whole_ref,
):
    me = lax.axis_index("tile")
    assemble(me, near_ref, far_ref, x_ref, 0)
    xhat = state_ref[:OWN, :]
    rstd = state_ref[OWN : OWN + 1, 0:1]
    gain = column(gain_ref[...])
    normed = xhat * gain + column(bias_ref[...])
    sig = jax.nn.sigmoid(normed)
    act = (normed * sig).astype(BF).astype(F32)
    for t, (dr, dc) in enumerate(TAPS):
        act_ref[OWN * t : OWN * (t + 1), :] = shifted(act, dr, dc).astype(BF)
    slope = sig * (1.0 + normed * (1.0 - sig))
    assemble(me, near_ref, far_ref, dy_ref, ROWS)
    xi = x_index()
    outs = (g0, g1, g2, g3)
    grad = dot(act_ref[...], dy_ref[...].reshape(POS, CH), 1, 0)
    split_blocks(xi, grad, whole_ref, outs, 9 * OWN + 16)
    for g in range(8):
        lanes = slice(128 * g, 128 * (g + 1))
        came = [w2_ref[4 * g + j].astype(F32) for j in range(4)]
        for t in range(8):
            rows, at = slice(OWN * (t // 4), OWN * (t // 4 + 1)), OWN * (t % 4)
            parts = [v[rows, at : at + OWN] for v in came]
            w2t_ref[OWN * t : OWN * (t + 1), lanes] = jnp.concatenate(parts, axis=1).astype(BF)
        parts = [jnp.concatenate([v[2 * OWN :, OWN * a : OWN * (a + 1)] for v in came], axis=1) for a in range(4)]
        w2t_ref[8 * OWN :, lanes] = jnp.concatenate(parts, axis=0).astype(BF)
    products = dot(w2t_ref[...], dy_ref[...].reshape(POS, CH), 1, 1)
    act_grad = jnp.zeros((OWN, POS), F32)
    for t, (dr, dc) in enumerate(TAPS):
        act_grad = act_grad + shifted(products[OWN * t : OWN * (t + 1)], -dr, -dc)
    norm_grad = act_grad * slope
    gain_sum = jnp.sum(norm_grad * xhat, axis=1, keepdims=True)
    shift_sum = jnp.sum(norm_grad, axis=1, keepdims=True)
    scaled = norm_grad * gain
    count = 1.0 / (OWN * POS)
    first_mean = jnp.sum(scaled, keepdims=True) * count
    second_mean = jnp.sum(scaled * xhat, keepdims=True) * count
    pre_grad = rstd * (scaled - first_mean - xhat * second_mean)
    pre_grad = pre_grad.astype(BF).astype(F32)
    for t, (dr, dc) in enumerate(TAPS):
        taps_ref[OWN * t : OWN * (t + 1), :] = shifted(pre_grad, -dr, -dc)
    taps = taps_ref[...]
    grad = dot(taps.astype(BF), x_ref[...].reshape(POS, CH), 1, 0)
    split_blocks(xi, grad, whole_ref, outs, 0)
    high_g = gain_sum.astype(BF).astype(F32)
    high_s = shift_sum.astype(BF).astype(F32)
    lane = lax.broadcasted_iota(jnp.int32, (OWN, 128), 1)
    sums = jnp.where(lane == 0, high_g, 0.0) + jnp.where(lane == 1, gain_sum - high_g, 0.0)
    sums = sums + jnp.where(lane == 2, high_s, 0.0) + jnp.where(lane == 3, shift_sum - high_s, 0.0)
    extra = sums.T[:16, :]
    rows = slice(9 * OWN, 9 * OWN + 16)
    for out in outs:
        out[rows, :] = jnp.zeros((16, 256), out.dtype)
        out[rows, :OWN] = extra.astype(out.dtype)
    rows_ref[...] = taps.T
    half = len(SUM_ORDER) // 2
    for part, out in enumerate((p_near, p_far)):
        blocks = []
        for mask in SUM_ORDER[part * half : (part + 1) * half]:
            start = pl.multiple_of((me ^ mask) * ROWS, ROWS)
            blocks.append(rows_ref[pl.ds(start, ROWS), :])
        out[...] = dot(jnp.concatenate(blocks, axis=0).astype(BF), w1_ref[...], 1, 0)


def split_blocks(xi, grad, whole_ref, outs, at):
    whole_ref[...] = grad
    rows = slice(at, at + grad.shape[0])
    for m, out in enumerate(outs):
        lane = pl.multiple_of((xi ^ m) * 256, 256)
        out[rows, :] = whole_ref[:, pl.ds(lane, 256)].astype(out.dtype)


def turn_kernel(w_ref, out_ref):
    turned = w_ref[...].astype(F32).T
    last = turned[:, 256:].reshape(32, 4, 8, OWN)
    last = jnp.concatenate([last[:, a] for a in range(4)], axis=2)
    low, high = turned[:, :128].reshape(32, OWN, 128), turned[:, 128:256].reshape(32, OWN, 128)
    out_ref[...] = jnp.concatenate([low, high, last], axis=1).astype(BF)


def finish_kernel(a0, a1, a2, a3, first_ref, second_ref, gain_ref, shift_ref):
    xi = x_index()
    sums = jnp.zeros((16, 256), F32)
    for m, part in enumerate((a0, a1, a2, a3)):
        lanes = pl.ds(pl.multiple_of((xi ^ m) * 256, 256), 256)
        first_ref[:, lanes] = part[: 9 * OWN, :].astype(F32)
        second_ref[:, lanes] = part[9 * OWN + 16 :, :].astype(F32)
        sums = jnp.where(xi == m, part[9 * OWN : 9 * OWN + 16, :].astype(F32), sums)
    gain_ref[...] = sums[0:1, :OWN] + sums[1:2, :OWN]
    shift_ref[...] = sums[2:3, :OWN] + sums[3:4, :OWN]


LIMIT = 14 * MB


def call(kernel, operands, outs, scratch=(), flops=0):
    vmem = pl.BlockSpec(memory_space=pltpu.VMEM)
    return pl.pallas_call(
        kernel,
        out_shape=[jax.ShapeDtypeStruct(s, d) for s, d in outs],
        in_specs=[vmem] * len(operands),
        out_specs=[vmem] * len(outs),
        scratch_shapes=[pltpu.VMEM(s, d) for s, d in scratch],
        compiler_params=pltpu.CompilerParams(vmem_limit_bytes=LIMIT),
        cost_estimate=pl.CostEstimate(flops=flops, bytes_accessed=4 * MB, transcendentals=0),
    )(*operands)


def resplit(total):
    gain = total[9 * OWN : 9 * OWN + 1] + total[9 * OWN + 1 : 9 * OWN + 2]
    shift = total[9 * OWN + 2 : 9 * OWN + 3] + total[9 * OWN + 3 : 9 * OWN + 4]
    high_g, high_s = gain.astype(BF).astype(F32), shift.astype(BF).astype(F32)
    row = lax.broadcasted_iota(jnp.int32, (16, 256), 0)
    extra = jnp.where(row == 0, high_g, 0.0) + jnp.where(row == 1, gain - high_g, 0.0)
    extra = extra + jnp.where(row == 2, high_s, 0.0) + jnp.where(row == 3, shift - high_s, 0.0)
    return extra.astype(BF)


def x_sum_kernel(own_ref, r1, r2, r3, out_ref):
    total = own_ref[...] + r1[...].astype(F32) + r2[...].astype(F32) + r3[...].astype(F32)
    out_ref[...] = total.astype(BF)
    out_ref[9 * OWN : 9 * OWN + 16, :] = resplit(total)


def z_sum_kernel(mine_ref, other_ref, out_ref):
    total = mine_ref[...].astype(F32) + other_ref[...].astype(F32)
    out_ref[...] = total.astype(BF)
    out_ref[9 * OWN : 9 * OWN + 16, :] = resplit(total)


def x_hops(parts):
    return [parts[0]] + [hop(parts[m], 2 * m, "sample", 8) for m in (1, 2, 3)]


def z_hop(mine):
    return hop(mine, 1, "sample", 8)


def spread(mine):
    return [mine] + [hop(mine, 2 * m, "sample", 8) for m in (1, 2, 3)]


def after(value, *others):
    return lax.optimization_barrier((value, *others))[0]


def per_device(inputs, first_weight, second_weight, norm_gain_vector, norm_bias, cotangent):
    w2 = second_weight.reshape(9 * OWN, CH)
    (turned,) = call(turn_kernel, [w2], [((32, 72, 128), BF)])
    block = jnp.concatenate([inputs.reshape(1, ROWS, CH), cotangent.reshape(1, ROWS, CH)], axis=1)
    held = jnp.concatenate([block] + [hop(block, m) for m in Z_MASKS])
    got = [hop(held, m) for m in Y_MASKS]
    w2_own = lax.all_to_all(after(turned, held), "tile", split_axis=0, concat_axis=0, tiled=True)
    near = jnp.concatenate([held] + got)
    far = hop(near, CORE)
    w1 = first_weight.reshape(9 * OWN, CH)
    gain, bias = norm_gain_vector.reshape(1, OWN), norm_bias.reshape(1, OWN)
    flops = 2 * 288 * POS * CH
    columns, taps, whole = (COLS, ROWS, CH), (9 * OWN, POS), (9 * OWN, CH)
    joint = (18 * OWN + 16, 256)
    (state,) = call(forward_kernel, [near, far, w1], [((OWN + 8, POS), F32)], [(columns, BF)], flops)
    conv_near, conv_far, *parts = call(
        main_kernel,
        [near, far, w2_own, w1, gain, bias, state],
        [((POS // 2, CH), F32)] * 2 + [(joint, F32)] + [(joint, BF)] * 3,
        [(columns, BF), (columns, BF), (taps, BF), (whole, BF), (taps, F32), ((POS, 9 * OWN), F32), (whole, F32)],
        4 * flops,
    )
    parts = x_hops(parts)
    conv_far = hop(conv_far, CORE)
    total = (conv_near + conv_far).reshape(4, POS // 8, CH)
    y_got = [hop(total[k].astype(BF), m) for k, m in zip((1, 2, 3), Y_MASKS)]
    (mine,) = call(x_sum_kernel, parts, [(joint, BF)])
    other = z_hop(mine)
    total = total[0] + y_got[0].astype(F32) + y_got[1].astype(F32) + y_got[2].astype(F32)
    total = after(total.reshape(4, ROWS, CH), other)
    z_got = [hop(total[k].astype(BF), m) for k, m in zip((1, 2, 3), Z_MASKS)]
    (summed,) = call(z_sum_kernel, [after(mine, *y_got), other], [(joint, BF)])
    blocks = spread(summed)
    total = total[0] + z_got[0].astype(F32) + z_got[1].astype(F32) + z_got[2].astype(F32)
    conv_back = total.astype(BF).astype(F32)
    input_grad = (cotangent.reshape(ROWS, CH).astype(F32) + conv_back).astype(BF)
    grad, row = ((9 * OWN, CH), F32), ((1, OWN), F32)
    first_grad, second_grad, gain_grad, shift_grad = call(finish_kernel, blocks, [grad, grad, row, row])
    return (
        input_grad.reshape(1, ROWS, 1, CH),
        first_grad.reshape(9, OWN, CH),
        jnp.transpose(second_grad.reshape(9, OWN, CH), (0, 2, 1)),
        gain_grad.reshape(OWN),
        shift_grad.reshape(OWN),
    )


def solution(mesh):
    return jax.shard_map(
        per_device,
        mesh=mesh,
        in_specs=(
            P("sample", None, "tile", None),
            P(None, "tile", None),
            P(None, "tile", None),
            P("tile"),
            P("tile"),
            P("sample", None, "tile", None),
        ),
        out_specs=(
            P("sample", None, "tile", None),
            P(None, "tile", None),
            P(None, None, "tile"),
            P("tile"),
            P("tile"),
        ),
        check_vma=False,
    )
```
